32 devices in a mesh: section: 2 (over x), dp: 4 (over z), tensor: 4 (over y, core).
Axes of the slice: x: 2, y: 2, z: 4, core: 2. Of those that a mesh axis runs over, the one named last changes fastest.
Arguments:
- tokens: bfloat16 [2, 4, 2048, 768], P(None, 'dp', 'tensor'), may hold values from -6 to 6
- segments: int32 [2, 4, 2048], P(None, 'dp'), may hold values from 0 to 7, never falling along the last dimension, each value on 1 to 800 neighbouring positions
- cotangent: bfloat16 [2, 4, 2048, 768], P(None, 'dp', 'tensor'), may hold values from -6 to 6
- ln1_gain: bfloat16 [2, 768], P('section', 'dp'), may hold values from 0.099609375 to 1.8984375
- ln1_shift: bfloat16 [2, 768], P('section', 'dp'), may hold values from -3 to 3
- qkv_weight: bfloat16 [2, 768, 3, 768], P('section', 'dp', None, 'tensor'), may hold values from -0.21875 to 0.21875
- qv_bias: bfloat16 [2, 2, 4, 192], P('section', None, 'tensor', 'dp'), may hold values from -2 to 2
- out_weight: bfloat16 [2, 768, 768], P('section', 'tensor', 'dp'), may hold values from -0.625 to 0.625
- out_bias: bfloat16 [2, 768], P('section', 'dp'), may hold values from -2 to 2
- ln2_gain: bfloat16 [2, 768], P('section', 'dp'), may hold values from 0.099609375 to 1.8984375
- ln2_shift: bfloat16 [2, 768], P('section', 'dp'), may hold values from -3 to 3
- up_weight: bfloat16 [2, 768, 3072], P('section', 'dp', 'tensor'), may hold values from -0.21875 to 0.21875
- up_bias: bfloat16 [2, 4, 768], P('section', 'tensor', 'dp'), may hold values from -2 to 2
- down_weight: bfloat16 [2, 3072, 768], P('section', 'tensor', 'dp'), may hold values from -0.15625 to 0.15625
- down_bias: bfloat16 [2, 768], P('section', 'dp'), may hold values from -2 to 2
Outputs:
- block_outputs: bfloat16 [2, 2, 4, 2048, 768], P('section', None, 'dp', 'tensor')
- input_grads: bfloat16 [2, 2, 4, 2048, 768], P('section', None, 'dp', 'tensor')
- grad_ln1_gain: float32 [2, 768], P('section', 'dp')
- grad_ln1_shift: float32 [2, 768], P('section', 'dp')
- grad_qkv_weight: float32 [2, 768, 3, 768], P('section', 'dp', None, 'tensor')
- grad_qv_bias: float32 [2, 2, 4, 192], P('section', None, 'tensor', 'dp')
- grad_out_weight: float32 [2, 768, 768], P('section', 'tensor', 'dp')
- grad_out_bias: float32 [2, 768], P('section', 'dp')
- grad_ln2_gain: float32 [2, 768], P('section', 'dp')
- grad_ln2_shift: float32 [2, 768], P('section', 'dp')
- grad_up_weight: float32 [2, 768, 3072], P('section', 'dp', 'tensor')
- grad_up_bias: float32 [2, 4, 768], P('section', 'tensor', 'dp')
- grad_down_weight: float32 [2, 3072, 768], P('section', 'tensor', 'dp')
- grad_down_bias: float32 [2, 768], P('section', 'dp')
The draws below stay inside these ranges and needn't reach their ends.
Inputs may be any that keep to these rules, and one draw needn't show every extreme that they name: `segments`: along each sequence the document numbers never fall; each document holds 1 to 800 tokens.
All inputs are finite; a program needn't handle non-finite values.
Results may differ from the reference program's by a relative error of at most 0.025.
Values may be sent and summed in bfloat16 or wider, within the bound.
No kernel may reach another device: no remote copies, remote signals or barrier semaphores. Data moves between devices by JAX's collectives and lax.ppermute only.
A program may use at most 256 MiB of HBM per device.

```python
import math
import jax
import jax.numpy as jnp
import numpy as np
from jax import lax

D = 768
HEADS = 12
HEAD_DIM = 64
FF = 3072
SEQ = 2048
MICRO = 2
DOCS = 8
DOC_MOST = 800
BATCH = 4
N_TENSOR = 4


def steps_of(rng, shape, pieces, low, top_value):
    level, own = 1.0, jax.random.fold_in(rng, 6)
    for axis_at, shards_of in pieces:
        draws = jnp.exp(jax.random.uniform(jax.random.fold_in(own, axis_at), (shards_of,), jnp.float32, low / len(pieces), top_value / len(pieces)))
        level = level * jnp.repeat(draws, shape[axis_at] // shards_of).reshape([-1 if axis == axis_at else 1 for axis in range(len(shape))])
    return level


def profile(number_of, total, bound, lean):
    weights = [(1 << 20) // math.isqrt(standing ** lean) + 1 for standing in range(2, number_of + 1)]
    rest, counts = total - bound - (number_of - 1), [1] * (number_of - 1)
    while rest > 0:
        candidates = [i for i in range(number_of - 1) if counts[i] < bound]
        whole, left = sum([weights[i] for i in candidates]), rest
        for i in candidates:
            extra = min(bound - counts[i], max(1, left * weights[i] // whole), rest)
            counts[i] = counts[i] + extra
            rest = rest - extra
    return np.array([bound] + counts)


def uneven(own_key, count, total, bound, slope):
    if count == 2:
        one = jax.random.randint(own_key, (), max(1, total - bound), min(bound, total - 1) + 1)
        return jnp.stack([one, total - one])
    sizes = jnp.asarray(profile(count, total, bound, slope), jnp.int32)
    couples = (count - 1) // 2
    source_of, taker = sizes[1:1 + 2 * couples:2], sizes[2:2 + 2 * couples:2]
    slack = jnp.minimum(source_of - 1, bound - taker)
    moved = jax.random.randint(jax.random.fold_in(own_key, 1), (couples,), 0, 1 << 20) % (slack + 1)
    sizes = sizes.at[1:1 + 2 * couples:2].set(source_of - moved).at[2:2 + 2 * couples:2].set(taker + moved)
    return sizes[jax.random.permutation(jax.random.fold_in(own_key, 2), count)]


def noise(stream_key, extent, width, bound, split=(), held_as=jnp.bfloat16):
    array = jax.random.normal(stream_key, extent, jnp.float32) * width
    if len(split) > 0:
        array = steps_of(stream_key, extent, split, -0.22, 0.18) * array
    return jnp.clip(array, min=-bound, max=bound).astype(held_as)


def setup_inputs(seed: int = 0) -> dict:
    streams_of = jax.random.split(jax.random.key(seed), 16)
    return {
        "tokens": noise(streams_of[0], (MICRO, BATCH, SEQ, D), 1.0, 6.0, ((1, 4), (2, 4))),
        "segments": jax.vmap(lambda own: jnp.searchsorted(jnp.cumsum(uneven(own, DOCS, SEQ, DOC_MOST, 0)), jnp.arange(SEQ), side="right"))(jax.random.split(streams_of[1], MICRO * BATCH)).reshape((MICRO, BATCH, SEQ)).astype(jnp.int32),
        "cotangent": noise(streams_of[2], (MICRO, BATCH, SEQ, D), 1.0, 6.0, ((1, 4), (2, 4))),
        "ln1_gain": jnp.clip(1.0 + 0.18 * jax.random.normal(streams_of[3], (2, D), jnp.float32), 0.099609375, 1.8984375).astype(jnp.bfloat16),
        "ln1_shift": noise(streams_of[4], (2, D), 0.5, 3.0, ((0, 2), (1, 4))),
        "qkv_weight": noise(streams_of[5], (2, D, 3, D), D ** -0.5, 0.21875, ((0, 2), (1, 4), (3, 4))),
        "qv_bias": noise(streams_of[6], (2, 2, N_TENSOR, D // N_TENSOR), 0.3, 2.0, ((0, 2), (2, 4), (3, 4))),
        "out_weight": noise(streams_of[7], (2, D, D), (D // 8) ** -0.5, 0.625, ((0, 2), (1, 4), (2, 4))),
        "out_bias": noise(streams_of[8], (2, D), 0.3, 2.0, ((0, 2), (1, 4))),
        "ln2_gain": jnp.clip(1.0 + 0.18 * jax.random.normal(streams_of[9], (2, D), jnp.float32), 0.099609375, 1.8984375).astype(jnp.bfloat16),
        "ln2_shift": noise(streams_of[10], (2, D), 0.5, 3.0, ((0, 2), (1, 4))),
        "up_weight": noise(streams_of[11], (2, D, FF), D ** -0.5, 0.21875, ((0, 2), (1, 4), (2, 4))),
        "up_bias": noise(streams_of[12], (2, N_TENSOR, FF // N_TENSOR), 0.3, 2.0, ((0, 2), (1, 4), (2, 4))),
        "down_weight": noise(streams_of[13], (2, FF, D), (FF // 2) ** -0.5, 0.15625, ((0, 2), (1, 4), (2, 4))),
        "down_bias": noise(streams_of[14], (2, D), 0.3, 2.0, ((0, 2), (1, 4))),
    }


highest = lax.Precision.HIGHEST
epsilon = 1e-05
query_rows = 512

@jax.custom_vjp
def low(v):
    return lax.optimization_barrier(v.astype(jnp.bfloat16)).astype(jnp.float32)

@jax.custom_vjp
def low_back(v):
    return v

def low_keep(v):
    return (low(v), None)

def low_pass(kept, grad):
    return (grad,)

def back_keep(v):
    return (v, None)

def back_low(kept, grad):
    return (low(grad),)
low.defvjp(low_keep, low_pass)
low_back.defvjp(back_keep, back_low)

def narrow_both(values):
    return low_back(low(values))

def layer_norm(rows_in, gain, offset):
    center = rows_in - lax.optimization_barrier(jnp.mean(rows_in, -1, keepdims=True))
    spread = lax.optimization_barrier(jnp.mean(center * center, -1, keepdims=True))
    return center * lax.rsqrt(spread + epsilon) * gain + offset

def gelu_tanh(inputs):
    return jax.nn.gelu(inputs, approximate=True)

def attention(queries, keys_all, values_all, seg_rows):
    length = queries.shape[0]
    block_len = min(query_rows, length)
    key_pos = jnp.arange(length, dtype=jnp.int32)
    scale = HEAD_DIM ** (-0.5)

    def one_block(block_index):
        row_start = (block_index * block_len).astype(jnp.int32)
        query_block = lax.dynamic_slice_in_dim(queries, row_start, block_len, 0)
        query_seg = lax.dynamic_slice_in_dim(seg_rows, row_start, block_len, 0)
        query_pos = row_start + jnp.arange(block_len, dtype=jnp.int32)
        logits = low_back(jnp.einsum('qhe,khe->hqk', query_block, keys_all, precision=highest) * scale)
        allowed = (query_pos[:, None] >= key_pos[None, :]) & (query_seg[:, None] == seg_rows[None, :])
        logits = jnp.where(allowed[None], logits, -1e+30)
        row_peak = lax.optimization_barrier(jnp.max(logits, -1, keepdims=True))
        exponent = jnp.exp(logits - row_peak)
        weights = low(exponent / lax.optimization_barrier(jnp.sum(exponent, -1, keepdims=True)))
        return jnp.einsum('hqk,khe->qhe', weights, values_all, precision=highest)
    mixed = lax.map(jax.checkpoint(one_block), jnp.arange(length // block_len, dtype=jnp.int32))
    return mixed.reshape(length, HEADS, HEAD_DIM)

def residual_block(rows_in, seg_rows, weights):
    norm1_gain, norm1_shift, qkv_mat, qv_vec, out_mat, out_vec, norm2_gain, norm2_shift, up_mat, up_vec, down_mat, down_vec = weights
    length = rows_in.shape[0]
    normed = low(layer_norm(rows_in, norm1_gain, norm1_shift))
    bias_rows = jnp.stack([qv_vec[0], jnp.zeros_like(qv_vec[0]), qv_vec[1]])
    projected = narrow_both(jnp.einsum('sd,dcf->scf', normed, qkv_mat, precision=highest) + bias_rows)
    queries = projected[:, 0].reshape(length, HEADS, HEAD_DIM)
    keys_all = projected[:, 1].reshape(length, HEADS, HEAD_DIM)
    values_all = projected[:, 2].reshape(length, HEADS, HEAD_DIM)
    mixed = narrow_both(attention(queries, keys_all, values_all, seg_rows).reshape(length, D))
    middle = rows_in + low_back(jnp.dot(mixed, out_mat, precision=highest) + out_vec)
    second = low(layer_norm(middle, norm2_gain, norm2_shift))
    hidden_pre = low_back(jnp.dot(second, up_mat, precision=highest) + up_vec)
    hidden = low(gelu_tanh(hidden_pre))
    return middle + low_back(jnp.dot(hidden, down_mat, precision=highest) + down_vec)

def reference(tokens, segments, cotangent, ln1_gain, ln1_shift, qkv_weight, qv_bias, out_weight, out_bias, ln2_gain, ln2_shift, up_weight, up_bias, down_weight, down_bias):
    seq_count = tokens.shape[1]
    flat_tokens = tokens.astype(jnp.float32).reshape(MICRO * seq_count, SEQ, D)
    flat_segments = segments.reshape(MICRO * seq_count, SEQ)
    flat_cotangent = cotangent.astype(jnp.float32).reshape(MICRO * seq_count, SEQ, D)
    params = (ln1_gain.astype(jnp.float32), ln1_shift.astype(jnp.float32), qkv_weight.astype(jnp.float32), qv_bias.astype(jnp.float32).reshape(2, 2, D), out_weight.astype(jnp.float32), out_bias.astype(jnp.float32), ln2_gain.astype(jnp.float32), ln2_shift.astype(jnp.float32), up_weight.astype(jnp.float32), up_bias.astype(jnp.float32).reshape(2, FF), down_weight.astype(jnp.float32), down_bias.astype(jnp.float32))
    probe_rows = jnp.zeros_like(flat_tokens)

    def forward(inputs, probes, weights):
        lower = tuple((member[0] for member in weights))
        upper = tuple((member[1] for member in weights))

        def per_sequence(packed):
            rows_in, seg_rows, added_rows = packed
            first_out = residual_block(rows_in, seg_rows, lower)
            second_out = residual_block(low_back(low(first_out)) + added_rows, seg_rows, upper)
            return (first_out, second_out)
        return lax.map(jax.checkpoint(per_sequence), (inputs, flat_segments, probes))
    outputs, pull = jax.vjp(forward, flat_tokens, probe_rows, params)
    grad_tokens, grad_probe, grad_params = pull((jnp.zeros_like(outputs[0]), flat_cotangent))
    block_outputs = jnp.stack([outputs[0], outputs[1]]).reshape(2, MICRO, seq_count, SEQ, D).astype(jnp.bfloat16)
    input_grads = jnp.stack([grad_tokens, grad_probe]).reshape(2, MICRO, seq_count, SEQ, D).astype(jnp.bfloat16)
    return (block_outputs, input_grads, grad_params[0], grad_params[1], grad_params[2], grad_params[3].reshape(2, 2, N_TENSOR, D // N_TENSOR), grad_params[4], grad_params[5], grad_params[6], grad_params[7], grad_params[8], grad_params[9].reshape(2, N_TENSOR, FF // N_TENSOR), grad_params[10], grad_params[11])
```

```python
import functools

import jax
import jax.numpy as jnp
from jax import lax
from jax.experimental import pallas as pl
from jax.experimental.pallas import tpu as pltpu
from jax.sharding import PartitionSpec as P

HEAD_DIM = 64
DOC_MOST = 800
EPSILON = 1e-05
TILE = 256
REMOTE_TILE = 160
REMOTE_ROWS = 800
MASKED = -1e30
VMEM_LIMIT = 48 * 1024 * 1024

CORE_SWAP = [(0, 1), (1, 0), (2, 3), (3, 2)]
CHIP_SWAP = [(0, 2), (2, 0), (1, 3), (3, 1)]
SECTION_SWAP = [(0, 1), (1, 0)]

f32 = jnp.float32
bf16 = jnp.bfloat16


def swap_core(v):
    return lax.ppermute(v, "tensor", CORE_SWAP)


def swap_chip(v):
    return lax.ppermute(v, "tensor", CHIP_SWAP)


def swap_section(v):
    return lax.ppermute(v, "section", SECTION_SWAP)


def shift_dp(v, by):
    n = lax.axis_size("dp")
    return lax.ppermute(v, "dp", [(i, (i + by) % n) for i in range(n)])


def assemble_kernel(place_ref, *refs):
    pieces, out_ref = refs[:-1], refs[-1]
    count, rows = len(pieces), pieces[0].shape[0]
    for k in range(count):
        at = pl.multiple_of(lax.rem(place_ref[0] + count - k, count) * rows, 16)
        out_ref[pl.ds(at, rows), :] = pieces[k][...]


def assemble(pieces, place):
    count = len(pieces)
    rows, columns = pieces[0].shape
    return pl.pallas_call(
        assemble_kernel,
        out_shape=jax.ShapeDtypeStruct((count * rows, columns), pieces[0].dtype),
        in_specs=[pl.BlockSpec(memory_space=pltpu.SMEM)]
        + [pl.BlockSpec(memory_space=pltpu.VMEM)] * count,
        out_specs=pl.BlockSpec(memory_space=pltpu.VMEM),
        name="assemble",
    )(place, *pieces)


def gather_dp(v, place):
    n = lax.axis_size("dp")
    if True:
        return lax.all_gather(v, "dp", axis=0, tiled=True)
    return assemble([v] + [shift_dp(v, k) for k in range(1, n)], place)


def scatter_dp(v):
    n = lax.axis_size("dp")
    if True:
        return lax.psum_scatter(v, "dp", scatter_dimension=0, tiled=True).astype(f32)
    rows = v.shape[0] // n
    place = lax.axis_index("dp")
    total = lax.dynamic_slice_in_dim(v, place * rows, rows, 0).astype(f32)
    for k in range(1, n):
        part = lax.dynamic_slice_in_dim(v, lax.rem(place + k, n) * rows, rows, 0)
        total = total + shift_dp(part, k).astype(f32)
    return total


def total_dp(v):
    n = lax.axis_size("dp")
    if True:
        return lax.psum(v, "dp")
    return v + shift_dp(v, 1) + shift_dp(v, 2) + shift_dp(v, 3)


def dot(a, b, dims):
    return lax.dot_general(a, b, (dims, ((), ())), preferred_element_type=f32)


ROWS_LAST = ((1,), (1,))
FIRST_FIRST = ((0,), (0,))
PLAIN = ((1,), (0,))


def tile_bias(seg_keys, seg_queries, key_at, query_at):
    shape = (seg_keys.shape[0], seg_queries.shape[1])
    key_pos = lax.broadcasted_iota(jnp.int32, shape, 0) + key_at
    query_pos = lax.broadcasted_iota(jnp.int32, shape, 1) + query_at
    allowed = (seg_keys == seg_queries) & (key_pos <= query_pos)
    return jnp.where(allowed, 0.0, MASKED).astype(f32)


def physical(tile, core):
    return pl.multiple_of(lax.rem(tile + 2 * core, 4) * TILE, TILE)


def head_columns(h, kind):
    at = kind * 192 + (h % 3) * HEAD_DIM
    return slice(at, at + HEAD_DIM)


def online_step(h, s, v, m_ref, l_ref, acc_ref):
    m_old = m_ref[h : h + 1, :]
    m_new = jnp.maximum(m_old, jnp.max(s, 0, keepdims=True))
    p = jnp.exp(s - m_new)
    alpha = jnp.exp(m_old - m_new)
    m_ref[h : h + 1, :] = m_new
    l_ref[h : h + 1, :] = l_ref[h : h + 1, :] * alpha + jnp.sum(p, 0, keepdims=True)
    rows = slice(h * HEAD_DIM, (h + 1) * HEAD_DIM)
    acc_ref[rows, :] = acc_ref[rows, :] * alpha + dot(v, p.astype(bf16), FIRST_FIRST)


def local_forward_kernel(
    info_ref, own_ref, oth_ref, seg_col_ref, seg_row_ref, acc_ref, m_ref, l_ref
):
    i = pl.program_id(0)
    core = info_ref[0]
    query_at = physical(i, core)
    m_ref[...] = jnp.full_like(m_ref, MASKED)
    l_ref[...] = jnp.zeros_like(l_ref)
    acc_ref[...] = jnp.zeros_like(acc_ref)

    def step(back, carry):
        j = i - back
        key_at = physical(j, core)
        j_pos = pl.multiple_of(j * TILE, TILE)
        bias = tile_bias(
            seg_col_ref[pl.ds(j_pos, TILE), :], seg_row_ref[...], j * TILE, i * TILE
        )
        for h in range(6):
            ref = own_ref if h < 3 else oth_ref
            q = ref[pl.ds(query_at, TILE), head_columns(h, 0)] * bf16(0.125)
            k = ref[pl.ds(key_at, TILE), head_columns(h, 1)]
            v = ref[pl.ds(key_at, TILE), head_columns(h, 2)]
            online_step(h, dot(k, q, ROWS_LAST) + bias, v, m_ref, l_ref, acc_ref)
        return carry

    lax.fori_loop(0, i - info_ref[1 + i] + 1, step, 0)


def remote_forward_kernel(
    info_ref,
    own_ref,
    oth_ref,
    kv_ref,
    seg_col_ref,
    seg_row_ref,
    acc_in,
    m_in,
    l_in,
    attn_ref,
    lse_ref,
    acc_ref,
    m_ref,
    l_ref,
):
    i = pl.program_id(0)
    core = info_ref[0]
    query_at = physical(i, core)
    m_ref[...] = m_in[...]
    l_ref[...] = l_in[...]
    acc_ref[...] = acc_in[...]

    def step(j, carry):
        key_at = pl.multiple_of(j * REMOTE_TILE, REMOTE_TILE)
        bias = tile_bias(
            seg_col_ref[pl.ds(key_at, REMOTE_TILE), :], seg_row_ref[...], 0, REMOTE_ROWS
        )
        for h in range(6):
            ref = own_ref if h < 3 else oth_ref
            q = ref[pl.ds(query_at, TILE), head_columns(h, 0)] * bf16(0.125)
            base = (h // 3) * 384 + (h % 3) * HEAD_DIM
            k = kv_ref[pl.ds(key_at, REMOTE_TILE), base : base + HEAD_DIM]
            v = kv_ref[pl.ds(key_at, REMOTE_TILE), base + 192 : base + 192 + HEAD_DIM]
            online_step(h, dot(k, q, ROWS_LAST) + bias, v, m_ref, l_ref, acc_ref)
        return carry

    lax.fori_loop(info_ref[5 + i], REMOTE_ROWS // REMOTE_TILE, step, 0)
    l = l_ref[0:6, :]
    lse_ref[0:6, :] = m_ref[0:6, :] + jnp.log(l)
    lse_ref[6:8, :] = jnp.zeros((2, TILE), f32)
    inverse = 1.0 / l
    for pair in range(3):
        rows = slice(pair * 128, pair * 128 + 128)
        top = acc_ref[pair * 128 : pair * 128 + 64, :] * inverse[2 * pair : 2 * pair + 1, :]
        low = acc_ref[pair * 128 + 64 : pair * 128 + 128, :] * inverse[2 * pair + 1 : 2 * pair + 2, :]
        attn_ref[:, rows] = jnp.concatenate([top, low], 0).T.astype(bf16)


def whole(shape):
    return pl.BlockSpec(shape, lambda i, info: (0,) * len(shape))


def position_block(rows):
    return pl.BlockSpec((rows, TILE), lambda i, info: (0, i))


def physical_block(columns):
    return pl.BlockSpec((TILE, columns), lambda i, info: (lax.rem(i + 2 * info[0], 4), 0))


PARAMS = pltpu.CompilerParams(
    vmem_limit_bytes=VMEM_LIMIT, dimension_semantics=("arbitrary",)
)


def local_forward(info, own, oth, seg_col, seg_row):
    rows = own.shape[0]
    return pl.pallas_call(
        local_forward_kernel,
        grid_spec=pltpu.PrefetchScalarGridSpec(
            num_scalar_prefetch=1,
            grid=(rows // TILE,),
            in_specs=[whole(own.shape), whole(oth.shape), whole(seg_col.shape), position_block(1)],
            out_specs=[position_block(384), position_block(8), position_block(8)],
        ),
        out_shape=[
            jax.ShapeDtypeStruct((384, rows), f32),
            jax.ShapeDtypeStruct((8, rows), f32),
            jax.ShapeDtypeStruct((8, rows), f32),
        ],
        compiler_params=PARAMS,
        name="attend_local",
    )(info, own, oth, seg_col, seg_row)


def remote_forward(info, own, oth, kv, seg_col, seg_row, acc, m, l):
    rows = own.shape[0]
    return pl.pallas_call(
        remote_forward_kernel,
        grid_spec=pltpu.PrefetchScalarGridSpec(
            num_scalar_prefetch=1,
            grid=(rows // TILE,),
            in_specs=[
                whole(own.shape),
                whole(oth.shape),
                whole(kv.shape),
                whole(seg_col.shape),
                position_block(1),
                position_block(384),
                position_block(8),
                position_block(8),
            ],
            out_specs=[physical_block(384), position_block(8)],
            scratch_shapes=[
                pltpu.VMEM((384, TILE), f32),
                pltpu.VMEM((8, TILE), f32),
                pltpu.VMEM((8, TILE), f32),
            ],
        ),
        out_shape=[
            jax.ShapeDtypeStruct((rows, 384), bf16),
            jax.ShapeDtypeStruct((8, rows), f32),
        ],
        compiler_params=PARAMS,
        name="attend_remote",
    )(info, own, oth, kv, seg_col, seg_row, acc, m, l)


def backward_step(q, k, v, go, lse, delta, bias):
    p = jnp.exp(dot(k, q, ROWS_LAST) + bias - lse)
    gp = dot(v, go, ROWS_LAST)
    gs = (p * (gp - delta)).astype(bf16)
    return dot(p.astype(bf16), go, PLAIN), dot(gs, q, PLAIN), dot(k, gs, FIRST_FIRST)


def remote_backward_kernel(
    info_ref,
    own_ref,
    oth_ref,
    kv_ref,
    seg_col_ref,
    seg_row_ref,
    go_ref,
    attn_ref,
    lse_ref,
    gkv_ref,
    gq_ref,
    delta_ref,
    gk_acc,
    gv_acc,
):
    i = pl.program_id(0)
    core = info_ref[0]
    query_at = physical(i, core)

    @pl.when(i == 0)
    def _():
        gk_acc[...] = jnp.zeros_like(gk_acc)
        gv_acc[...] = jnp.zeros_like(gv_acc)

    for pair in range(3):
        columns = slice(pair * 128, pair * 128 + 128)
        product = (go_ref[:, columns].astype(f32) * attn_ref[:, columns].astype(f32)).T
        for half in range(2):
            delta_ref[2 * pair + half : 2 * pair + half + 1, :] = jnp.sum(
                product[half * 64 : half * 64 + 64], 0, keepdims=True
            )
    delta_ref[6:8, :] = jnp.zeros((2, TILE), f32)
    gq_ref[...] = jnp.zeros_like(gq_ref)

    def step(j, carry):
        key_at = pl.multiple_of(j * REMOTE_TILE, REMOTE_TILE)
        rows = pl.ds(key_at, REMOTE_TILE)
        bias = tile_bias(seg_col_ref[rows, :], seg_row_ref[...], 0, REMOTE_ROWS)
        for h in range(6):
            ref = own_ref if h < 3 else oth_ref
            q = ref[pl.ds(query_at, TILE), head_columns(h, 0)] * bf16(0.125)
            base = (h // 3) * 384 + (h % 3) * HEAD_DIM
            k = kv_ref[rows, base : base + HEAD_DIM]
            v = kv_ref[rows, base + 192 : base + 192 + HEAD_DIM]
            go = go_ref[:, h * HEAD_DIM : (h + 1) * HEAD_DIM]
            gv, gk, gq = backward_step(
                q, k, v, go, lse_ref[h : h + 1, :], delta_ref[h : h + 1, :], bias
            )
            gv_acc[h, rows, :] += gv
            gk_acc[h, rows, :] += gk
            gq_ref[h * HEAD_DIM : (h + 1) * HEAD_DIM, :] += gq
        return carry

    lax.fori_loop(info_ref[5 + i], REMOTE_ROWS // REMOTE_TILE, step, 0)

    @pl.when(i == pl.num_programs(0) - 1)
    def _():
        for h in range(6):
            base = (h // 3) * 384 + (h % 3) * HEAD_DIM
            gkv_ref[:, base : base + HEAD_DIM] = gk_acc[h].astype(bf16)
            gkv_ref[:, base + 192 : base + 192 + HEAD_DIM] = gv_acc[h].astype(bf16)


def remote_backward(info, own, oth, kv, seg_col, seg_row, go, attn, lse):
    rows = own.shape[0]
    return pl.pallas_call(
        remote_backward_kernel,
        grid_spec=pltpu.PrefetchScalarGridSpec(
            num_scalar_prefetch=1,
            grid=(rows // TILE,),
            in_specs=[
                whole(own.shape),
                whole(oth.shape),
                whole(kv.shape),
                whole(seg_col.shape),
                position_block(1),
                physical_block(384),
                physical_block(384),
                position_block(8),
            ],
            out_specs=[whole(kv.shape), position_block(384), position_block(8)],
            scratch_shapes=[
                pltpu.VMEM((6, REMOTE_ROWS, HEAD_DIM), f32),
                pltpu.VMEM((6, REMOTE_ROWS, HEAD_DIM), f32),
            ],
        ),
        out_shape=[
            jax.ShapeDtypeStruct(kv.shape, bf16),
            jax.ShapeDtypeStruct((384, rows), f32),
            jax.ShapeDtypeStruct((8, rows), f32),
        ],
        compiler_params=PARAMS,
        name="attend_remote_back",
    )(info, own, oth, kv, seg_col, seg_row, go, attn, lse)


def local_backward_kernel(
    info_ref,
    own_ref,
    oth_ref,
    seg_col_ref,
    seg_row_ref,
    go_ref,
    lse_ref,
    delta_ref,
    gq_in,
    gown_ref,
    goth_ref,
    gq_acc,
    gk_acc,
    gv_acc,
):
    i = pl.program_id(0)
    core = info_ref[0]
    query_at = physical(i, core)

    @pl.when(i == 0)
    def _():
        gk_acc[...] = jnp.zeros_like(gk_acc)
        gv_acc[...] = jnp.zeros_like(gv_acc)

    gq_acc[...] = gq_in[...]

    def step(back, carry):
        j = i - back
        rows = pl.ds(physical(j, core), TILE)
        j_pos = pl.multiple_of(j * TILE, TILE)
        bias = tile_bias(
            seg_col_ref[pl.ds(j_pos, TILE), :], seg_row_ref[...], j * TILE, i * TILE
        )
        for h in range(6):
            ref = own_ref if h < 3 else oth_ref
            q = ref[pl.ds(query_at, TILE), head_columns(h, 0)] * bf16(0.125)
            k = ref[rows, head_columns(h, 1)]
            v = ref[rows, head_columns(h, 2)]
            go = go_ref[:, h * HEAD_DIM : (h + 1) * HEAD_DIM]
            gv, gk, gq = backward_step(
                q, k, v, go, lse_ref[h : h + 1, :], delta_ref[h : h + 1, :], bias
            )
            gv_acc[h, rows, :] += gv
            gk_acc[h, rows, :] += gk
            gq_acc[h * HEAD_DIM : (h + 1) * HEAD_DIM, :] += gq
        return carry

    lax.fori_loop(0, i - info_ref[1 + i] + 1, step, 0)
    for h in range(6):
        out = gown_ref if h < 3 else goth_ref
        block = gq_acc[h * HEAD_DIM : (h + 1) * HEAD_DIM, :].T * 0.125
        out[pl.ds(query_at, TILE), head_columns(h, 0)] = block.astype(bf16)

    @pl.when(i == pl.num_programs(0) - 1)
    def _():
        for h in range(6):
            out = gown_ref if h < 3 else goth_ref
            out[:, head_columns(h, 1)] = gk_acc[h].astype(bf16)
            out[:, head_columns(h, 2)] = gv_acc[h].astype(bf16)


def local_backward(info, own, oth, seg_col, seg_row, go, lse, delta, gq):
    rows = own.shape[0]
    return pl.pallas_call(
        local_backward_kernel,
        grid_spec=pltpu.PrefetchScalarGridSpec(
            num_scalar_prefetch=1,
            grid=(rows // TILE,),
            in_specs=[
                whole(own.shape),
                whole(oth.shape),
                whole(seg_col.shape),
                position_block(1),
                physical_block(384),
                position_block(8),
                position_block(8),
                position_block(384),
            ],
            out_specs=[whole(own.shape), whole(oth.shape)],
            scratch_shapes=[
                pltpu.VMEM((384, TILE), f32),
                pltpu.VMEM((6, rows, HEAD_DIM), f32),
                pltpu.VMEM((6, rows, HEAD_DIM), f32),
            ],
        ),
        out_shape=[
            jax.ShapeDtypeStruct(own.shape, bf16),
            jax.ShapeDtypeStruct(oth.shape, bf16),
        ],
        compiler_params=PARAMS,
        name="attend_local_back",
    )(info, own, oth, seg_col, seg_row, go, lse, delta, gq)


def normalize(v):
    center = v - jnp.mean(v, -1, keepdims=True)
    scale = lax.rsqrt(jnp.mean(center * center, -1, keepdims=True) + EPSILON)
    return center * scale, scale


def normalize_back(v, gain, grad):
    unit, scale = normalize(v)
    scaled = grad * gain
    back = scale * (
        scaled
        - jnp.mean(scaled, -1, keepdims=True)
        - unit * jnp.mean(scaled * unit, -1, keepdims=True)
    )
    return back, jnp.sum(grad * unit, 0), jnp.sum(grad, 0)


def both_rows(own):
    return jnp.concatenate([own, swap_core(own)], 0)


def split_sum(parts):
    half = parts[0][0].shape[0] // 2

    def partial(rows):
        return sum(dot(a[rows], b, ROWS_LAST) for a, b in parts)

    received = swap_core(partial(slice(half, None)).astype(bf16))
    return partial(slice(0, half)) + received.astype(f32)


def gelu_and_slope(v):
    c, a = 0.7978845608028654, 0.044715
    t = jnp.tanh(c * (v + a * v * v * v))
    half = 0.5 * (1.0 + t)
    slope = half + 0.5 * v * (1.0 - t * t) * (c * (1.0 + 3.0 * a * v * v))
    return v * half, slope


def block_forward(h, masks, weights, vectors):
    info, seg_col, seg_row, seg_far_col, is_first_core = masks
    qkv, out, up, down = weights
    ln1_gain, ln1_shift, out_bias, ln2_gain, ln2_shift, down_bias, qkv_bias, up_bias = vectors
    normed = both_rows((normalize(h)[0] * ln1_gain + ln1_shift).astype(bf16))
    proj = [(dot(normed, qkv[n], PLAIN) + qkv_bias[n]).astype(bf16) for n in range(2)]
    half = normed.shape[0] // 2
    keys = jnp.concatenate([proj[1][:, 192:], proj[0][:, 192:]], 1)
    first = jnp.where(is_first_core, keys[:half], keys[half:])
    second = jnp.where(is_first_core, keys[half:], keys[:half])
    sent = jnp.concatenate([first[half - (REMOTE_ROWS - half) :], second], 0)
    far = lax.ppermute(sent, "tensor", [(0, 2), (1, 3)])
    state = local_forward(info, proj[0], proj[1], seg_col, seg_row)
    attn, lse = remote_forward(info, proj[0], proj[1], far, seg_far_col, seg_row, *state)
    middle = h + (split_sum([(attn[:, :192], out[0]), (attn[:, 192:], out[1])]) + out_bias)
    second = both_rows((normalize(middle)[0] * ln2_gain + ln2_shift).astype(bf16))
    hidden, slopes = [], []
    for n in range(2):
        value, slope = gelu_and_slope(dot(second, up[n], PLAIN) + up_bias[n])
        hidden.append(value.astype(bf16))
        slopes.append(slope.astype(bf16))
    result = middle + (split_sum([(hidden[0], down[0]), (hidden[1], down[1])]) + down_bias)
    return result, (h, middle, normed, proj, far, attn, lse, second, hidden, slopes)


def block_backward(gy, masks, saved, weights, vectors):
    info, seg_col, seg_row, seg_far_col, is_first_core = masks
    qkv, out, up, down = weights
    ln1_gain, ln2_gain = vectors[0], vectors[3]
    h, middle, normed, proj, far, attn, lse, second, hidden, slopes = saved
    gyr = gy.astype(bf16)
    g_down_bias = jnp.sum(gyr.astype(f32), 0)
    wide = both_rows(gyr)
    gpre = [(dot(wide, down[n], PLAIN) * slopes[n].astype(f32)).astype(bf16) for n in range(2)]
    g_up_bias = [jnp.sum(g.astype(f32), 0) for g in gpre]
    gsecond = split_sum([(gpre[0], up[0]), (gpre[1], up[1])])
    g_down = [dot(wide, hidden[n], FIRST_FIRST).astype(bf16) for n in range(2)]
    g_up = [dot(second, gpre[n], FIRST_FIRST).astype(bf16) for n in range(2)]
    gmid_n, g_ln2_gain, g_ln2_shift = normalize_back(middle, ln2_gain, gsecond)
    gmid = gy + gmid_n
    gmr = gmid.astype(bf16)
    g_out_bias = jnp.sum(gmr.astype(f32), 0)
    mid_wide = both_rows(gmr)
    gattn = jnp.concatenate([dot(mid_wide, out[n], PLAIN).astype(bf16) for n in range(2)], 1)
    g_out = [
        dot(mid_wide, attn[:, n * 192 : n * 192 + 192], FIRST_FIRST).astype(bf16) for n in range(2)
    ]
    gfar, gq, delta = remote_backward(
        info, proj[0], proj[1], far, seg_far_col, seg_row, gattn, attn, lse
    )
    gnear = lax.ppermute(gfar, "tensor", [(2, 0), (3, 1)])
    gproj = local_backward(info, proj[0], proj[1], seg_col, seg_row, gattn, lse, delta, gq)
    half = normed.shape[0] // 2
    gnear = jnp.pad(gnear, ((2 * half - REMOTE_ROWS, 0), (0, 0)))
    gnear = jnp.concatenate(
        [
            jnp.where(is_first_core, gnear[:half], gnear[half:]),
            jnp.where(is_first_core, gnear[half:], gnear[:half]),
        ],
        0,
    )
    gproj = [
        (gproj[n].astype(f32) + jnp.pad(gnear[:, at : at + 384].astype(f32), ((0, 0), (192, 0))))
        .astype(bf16)
        for n, at in ((0, 384), (1, 0))
    ]
    g_qkv_bias = [jnp.sum(g.astype(f32), 0) for g in gproj]
    g_qkv = [dot(normed, gproj[n], FIRST_FIRST).astype(bf16) for n in range(2)]
    gnormed = split_sum([(gproj[0], qkv[0]), (gproj[1], qkv[1])])
    gh_n, g_ln1_gain, g_ln1_shift = normalize_back(h, ln1_gain, gnormed)
    rows_grads = (g_ln1_gain, g_ln1_shift, g_out_bias, g_ln2_gain, g_ln2_shift, g_down_bias)
    return gmid + gh_n, (g_qkv, g_out, g_up, g_down), rows_grads, (g_qkv_bias, g_up_bias)


def fetch_weight(slab, place):
    full = gather_dp(slab, place)
    return full, swap_chip(full)


def reduce_weight(grads):
    return scatter_dp((grads[0].astype(f32) + swap_chip(grads[1]).astype(f32)).astype(bf16))


def body(
    tokens,
    segments,
    cotangent,
    ln1_gain,
    ln1_shift,
    qkv_weight,
    qv_bias,
    out_weight,
    out_bias,
    ln2_gain,
    ln2_shift,
    up_weight,
    up_bias,
    down_weight,
    down_bias,
):
    section = lax.axis_index("section")
    is_leading = section == 0
    tensor = lax.axis_index("tensor")
    core = lax.rem(tensor, 2)
    chip = tensor // 2
    dp = lax.axis_index("dp")
    dp_size = lax.axis_size("dp")
    place = dp.astype(jnp.int32).reshape(1)
    share = ln1_gain.shape[1]
    features = share * dp_size
    local_width = qkv_weight.shape[3]
    local_units = up_weight.shape[2]

    row = jnp.concatenate(
        [
            ln1_gain[0],
            ln1_shift[0],
            out_bias[0],
            ln2_gain[0],
            ln2_shift[0],
            down_bias[0],
            qv_bias[0].reshape(-1),
            up_bias[0].reshape(-1),
        ]
    )[None]
    other_row = swap_section(row)
    rows = jnp.where(
        is_leading, jnp.concatenate([row, other_row], 1), jnp.concatenate([other_row, row], 1)
    )
    rows = jnp.concatenate([rows, swap_chip(rows)], 1)
    if dp_size == 4:
        pieces = [rows] + [shift_dp(rows, k) for k in range(1, dp_size)]
        rows = jnp.zeros((dp_size,) + rows.shape[1:], rows.dtype)
        for k in range(dp_size):
            rows = lax.dynamic_update_slice_in_dim(
                rows, pieces[k], lax.rem(dp + dp_size - k, dp_size), 0
            )
    else:
        rows = lax.all_gather(rows, "dp", axis=0, tiled=True)
    length = row.shape[1]
    rows = rows.reshape(dp_size, 2, 2, length).astype(f32)
    qv_share = local_width // dp_size
    up_share = local_units // dp_size

    def vectors_of(b):
        plain = [rows[:, 0, b, n * share : (n + 1) * share].reshape(-1) for n in range(6)]
        qkv_bias, up_biases = [], []
        for n in range(2):
            at = 6 * share
            query = rows[:, n, b, at : at + qv_share].reshape(-1)
            value = rows[:, n, b, at + qv_share : at + 2 * qv_share].reshape(-1)
            qkv_bias.append(jnp.concatenate([query, jnp.zeros_like(query), value]))
            up_biases.append(rows[:, n, b, at + 2 * qv_share :].reshape(-1))
        return tuple(plain) + (qkv_bias, up_biases)

    vectors = [vectors_of(b) for b in range(2)]

    slabs = (
        qkv_weight[0].reshape(share, 3 * local_width),
        out_weight[0].T,
        up_weight[0],
        down_weight[0].T,
    )
    others = tuple(swap_section(s) for s in slabs)
    weights = []
    for b in range(2):
        weights.append(
            tuple(
                fetch_weight(jnp.where(section == b, own, other), place)
                for own, other in zip(slabs, others)
            )
        )

    seg = jnp.where(is_leading, segments[0, 0], segments[1, 0])
    near_len = seg.shape[0] // 2
    seg_near = lax.dynamic_slice_in_dim(seg, chip * near_len, near_len, 0)
    seg_far = seg[near_len - REMOTE_ROWS : near_len]
    heads_of = seg_near[::TILE]
    start = jnp.sum((seg_near[None, :] < heads_of[:, None]).astype(jnp.int32), 1)
    far_start = jnp.sum((seg_far < seg_far[-1]).astype(jnp.int32))
    crosses = (heads_of == seg_far[-1]) & (chip == 1)
    info = jnp.concatenate(
        [
            core.astype(jnp.int32).reshape(1),
            start // TILE,
            jnp.where(crosses, far_start // REMOTE_TILE, REMOTE_ROWS // REMOTE_TILE),
        ]
    ).astype(jnp.int32)
    masks = (info, seg_near[:, None], seg_near[None, :], seg_far[:, None], core == 0)

    h = jnp.where(is_leading, tokens[0, 0], tokens[1, 0]).astype(f32)
    outs, saved = [], []
    for b in range(2):
        result, kept = block_forward(h, masks, weights[b], vectors[b])
        outs.append(result.astype(bf16))
        saved.append(kept)
        h = outs[b].astype(f32)

    gy = jnp.where(is_leading, cotangent[0, 0], cotangent[1, 0]).astype(f32)
    back = [None, None]
    reduced = [None, None]
    row_grads = [None, None]
    unit_grads = [None, None]
    for b in (1, 0):
        grad_input, grads, row_grads[b], unit_grads[b] = block_backward(
            gy, masks, saved[b], weights[b], vectors[b]
        )
        back[b] = grad_input.astype(bf16)
        reduced[b] = [reduce_weight(g) for g in grads]
        gy = back[b].astype(f32)

    def to_owner(pair):
        keep = jnp.where(is_leading, pair[0], pair[1])
        give = jnp.where(is_leading, pair[1], pair[0])
        return keep + swap_section(give.astype(bf16)).astype(f32)

    g_qkv, g_out, g_up, g_down = [to_owner((reduced[0][n], reduced[1][n])) for n in range(4)]

    plain = jnp.stack([jnp.concatenate(row_grads[b]) for b in range(2)])
    plain = plain + swap_core(plain)
    units = [
        jnp.stack([jnp.concatenate([unit_grads[b][0][n], unit_grads[b][1][n]]) for b in range(2)])
        for n in range(2)
    ]
    swapped = swap_chip(jnp.concatenate([plain, units[1]], 1))
    plain_width = plain.shape[1]
    total = jnp.concatenate([plain, units[0]], 1) + swapped
    total = total_dp(total)
    keep = jnp.where(is_leading, total[0], total[1])
    give = jnp.where(is_leading, total[1], total[0])
    total = keep + swap_section(give[None])[0]

    def mine(vector):
        part = vector.shape[0] // dp_size
        return lax.dynamic_slice_in_dim(vector, dp * part, part, 0)

    shares = [mine(total[n * features : (n + 1) * features]) for n in range(6)]
    unit_total = total[plain_width:]
    g_query = mine(unit_total[:local_width])
    g_value = mine(unit_total[2 * local_width : 3 * local_width])
    g_up_bias = mine(unit_total[3 * local_width :])

    def exchanged(pair):
        own = jnp.where(is_leading, pair[0], pair[1])
        other = swap_section(jnp.where(is_leading, pair[1], pair[0]))
        return jnp.stack(
            [jnp.where(is_leading, own, other), jnp.where(is_leading, other, own)]
        )[None, :, None]

    return (
        exchanged(outs),
        exchanged(back),
        shares[0][None],
        shares[1][None],
        g_qkv.reshape(1, share, 3, local_width),
        jnp.stack([g_query, g_value])[None, :, None],
        g_out.T[None],
        shares[2][None],
        shares[3][None],
        shares[4][None],
        g_up[None],
        g_up_bias[None, None],
        g_down.T[None],
        shares[5][None],
    )


def solution(mesh):
    placed = (
        P(None, "dp", "tensor", None),
        P(None, "dp", None),
        P(None, "dp", "tensor", None),
        P("section", "dp"),
        P("section", "dp"),
        P("section", "dp", None, "tensor"),
        P("section", None, "tensor", "dp"),
        P("section", "tensor", "dp"),
        P("section", "dp"),
        P("section", "dp"),
        P("section", "dp"),
        P("section", "dp", "tensor"),
        P("section", "tensor", "dp"),
        P("section", "tensor", "dp"),
        P("section", "dp"),
    )
    return jax.shard_map(
        body,
        mesh=mesh,
        in_specs=placed,
        out_specs=(
            P("section", None, "dp", "tensor", None),
            P("section", None, "dp", "tensor", None),
            P("section", "dp"),
            P("section", "dp"),
            P("section", "dp", None, "tensor"),
            P("section", None, "tensor", "dp"),
            P("section", "tensor", "dp"),
            P("section", "dp"),
            P("section", "dp"),
            P("section", "dp"),
            P("section", "dp", "tensor"),
            P("section", "tensor", "dp"),
            P("section", "tensor", "dp"),
            P("section", "dp"),
        ),
        check_vma=False,
    )
```

```python
import functools

import jax
import jax.numpy as jnp
from jax import lax
from jax.experimental import pallas as pl
from jax.experimental.pallas import tpu as pltpu
from jax.sharding import PartitionSpec as P

HEAD_DIM = 64
DOC_MOST = 800
EPSILON = 1e-05
TILE = 256
REMOTE_TILE = 160
REMOTE_ROWS = 800
MASKED = -1e30
VMEM_LIMIT = 48 * 1024 * 1024

CORE_SWAP = [(0, 1), (1, 0), (2, 3), (3, 2)]
CHIP_SWAP = [(0, 2), (2, 0), (1, 3), (3, 1)]
SECTION_SWAP = [(0, 1), (1, 0)]

f32 = jnp.float32
bf16 = jnp.bfloat16


SECTION, DP, TENSOR = "section", "dp", "tensor"


class K:
    (
        ROWS,
        SENT,
        ATTEND,
        FAR,
        MIDDLE,
        SECOND,
        HIDDEN,
        GPRE,
        DOWN,
        UP,
        GMR,
        OUT,
        GPROJ,
        QKV,
        MARK,
        GNORMED,
        FIRST,
        PICK,
        DP,
        CHIP,
        SECTION,
        ALL,
        BACK,
        GSECTION,
        GCHIP,
        UNITS,
        HEADS,
        GDP,
    ) = range(28)


def swap_core(v):
    return lax.ppermute(v, TENSOR, CORE_SWAP)


def swap_chip(v):
    return lax.ppermute(v, TENSOR, CHIP_SWAP)


def swap_section(v):
    return lax.ppermute(v, SECTION, SECTION_SWAP)


def shift_dp(v, by):
    n = lax.axis_size(DP)
    return lax.ppermute(v, DP, [(i, (i + by) % n) for i in range(n)])


def gather_dp(v):
    return lax.all_gather(v, DP, axis=0, tiled=True)


def scatter_dp(v):
    return lax.psum_scatter(v, DP, scatter_dimension=0, tiled=True)


def total_dp(v):
    n = lax.axis_size(DP)
    if n != 4:
        return lax.psum(v, DP)
    return v + shift_dp(v, 1) + shift_dp(v, 2) + shift_dp(v, 3)


def after(value, *others):
    return lax.optimization_barrier((value, others))[0]


def dot(a, b, dims):
    return lax.dot_general(a, b, (dims, ((), ())), preferred_element_type=f32)


ROWS_LAST = ((1,), (1,))
FIRST_FIRST = ((0,), (0,))
PLAIN = ((1,), (0,))


def tile_bias(seg_keys, seg_queries, key_at, query_at):
    shape = (seg_keys.shape[0], seg_queries.shape[1])
    key_pos = lax.broadcasted_iota(jnp.int32, shape, 0) + key_at
    query_pos = lax.broadcasted_iota(jnp.int32, shape, 1) + query_at
    allowed = (seg_keys == seg_queries) & (key_pos <= query_pos)
    return jnp.where(allowed, 0.0, MASKED).astype(f32)


def physical(tile, core):
    return pl.multiple_of(lax.rem(tile + 2 * core, 4) * TILE, TILE)


def head_columns(h, kind):
    at = kind * 192 + (h % 3) * HEAD_DIM
    return slice(at, at + HEAD_DIM)


def online_step(h, s, v, m_ref, l_ref, acc_ref):
    m_old = m_ref[h : h + 1, :]
    m_new = jnp.maximum(m_old, jnp.max(s, 0, keepdims=True))
    p = jnp.exp(s - m_new)
    alpha = jnp.exp(m_old - m_new)
    m_ref[h : h + 1, :] = m_new
    l_ref[h : h + 1, :] = l_ref[h : h + 1, :] * alpha + jnp.sum(p, 0, keepdims=True)
    rows = slice(h * HEAD_DIM, (h + 1) * HEAD_DIM)
    acc_ref[rows, :] = acc_ref[rows, :] * alpha + dot(v, p.astype(bf16), FIRST_FIRST)


def local_forward_kernel(
    info_ref, own_ref, oth_ref, seg_col_ref, seg_row_ref, acc_ref, m_ref, l_ref
):
    i = pl.program_id(0)
    core = info_ref[0]
    query_at = physical(i, core)
    m_ref[...] = jnp.full_like(m_ref, MASKED)
    l_ref[...] = jnp.zeros_like(l_ref)
    acc_ref[...] = jnp.zeros_like(acc_ref)

    def step(back, carry):
        j = i - back
        key_at = physical(j, core)
        j_pos = pl.multiple_of(j * TILE, TILE)
        bias = tile_bias(
            seg_col_ref[pl.ds(j_pos, TILE), :], seg_row_ref[...], j * TILE, i * TILE
        )
        for h in range(6):
            ref = own_ref if h < 3 else oth_ref
            q = ref[pl.ds(query_at, TILE), head_columns(h, 0)] * bf16(0.125)
            k = ref[pl.ds(key_at, TILE), head_columns(h, 1)]
            v = ref[pl.ds(key_at, TILE), head_columns(h, 2)]
            online_step(h, dot(k, q, ROWS_LAST) + bias, v, m_ref, l_ref, acc_ref)
        return carry

    lax.fori_loop(0, i - info_ref[1 + i] + 1, step, 0)


def remote_forward_kernel(
    out_at,
    info_ref,
    own_ref,
    oth_ref,
    kv_ref,
    seg_col_ref,
    seg_row_ref,
    acc_in,
    m_in,
    l_in,
    first_ref,
    second_ref,
    attn_ref,
    lse_ref,
    part_ref,
    sent_ref,
    acc_ref,
    m_ref,
    l_ref,
):
    block = pl.program_id(0)
    i = lax.rem(block + 2 * info_ref[0], 4)
    query_at = pl.multiple_of(block * TILE, TILE)
    m_ref[...] = m_in[...]
    l_ref[...] = l_in[...]
    acc_ref[...] = acc_in[...]

    def step(j, carry):
        key_at = pl.multiple_of(j * REMOTE_TILE, REMOTE_TILE)
        bias = tile_bias(
            seg_col_ref[pl.ds(key_at, REMOTE_TILE), :], seg_row_ref[...], 0, REMOTE_ROWS
        )
        for h in range(6):
            ref = own_ref if h < 3 else oth_ref
            q = ref[pl.ds(query_at, TILE), head_columns(h, 0)] * bf16(0.125)
            base = (h // 3) * 384 + (h % 3) * HEAD_DIM
            k = kv_ref[pl.ds(key_at, REMOTE_TILE), base : base + HEAD_DIM]
            v = kv_ref[pl.ds(key_at, REMOTE_TILE), base + 192 : base + 192 + HEAD_DIM]
            online_step(h, dot(k, q, ROWS_LAST) + bias, v, m_ref, l_ref, acc_ref)
        return carry

    lax.fori_loop(info_ref[5 + i], REMOTE_ROWS // REMOTE_TILE, step, 0)
    l = l_ref[0:6, :]
    lse_ref[0:6, :] = m_ref[0:6, :] + jnp.log(l)
    lse_ref[6:8, :] = jnp.zeros((2, TILE), f32)
    inverse = 1.0 / l
    for pair in range(3):
        rows = slice(pair * 128, pair * 128 + 128)
        top = acc_ref[pair * 128 : pair * 128 + 64, :] * inverse[2 * pair : 2 * pair + 1, :]
        low = acc_ref[pair * 128 + 64 : pair * 128 + 128, :] * inverse[2 * pair + 1 : 2 * pair + 2, :]
        attn_ref[:, rows] = jnp.concatenate([top, low], 0).T.astype(bf16)
    total = dot(attn_ref[:, 0:192], first_ref[:, out_at[0] : out_at[0] + 192], ROWS_LAST)
    total += dot(attn_ref[:, 192:384], second_ref[:, out_at[1] : out_at[1] + 192], ROWS_LAST)
    store_rows(block, total, part_ref, sent_ref)


def rows_of(block, kept_ref, other_ref):
    return jnp.where(block < 2, kept_ref[...], other_ref[...])


def store_rows(block, total, part_ref, sent_ref):
    half = pl.num_programs(0) // 2

    @pl.when(block < half)
    def _():
        part_ref[...] = total

    @pl.when(block >= half)
    def _():
        sent_ref[...] = total.astype(bf16)


def whole(shape):
    return pl.BlockSpec(shape, lambda i, info: (0,) * len(shape))


def position_block(rows):
    return pl.BlockSpec((rows, TILE), lambda i, info: (0, i))


def physical_block(columns):
    return pl.BlockSpec((TILE, columns), lambda i, info: (lax.rem(i + 2 * info[0], 4), 0))


def tile_of(columns):
    return pl.BlockSpec((TILE, columns), lambda i, *info: (i, 0))


def fixed(shape):
    return pl.BlockSpec(shape, lambda i, *info: (0,) * len(shape))


KEPT_ROWS = pl.BlockSpec((TILE, 768), lambda i, *info: (jnp.minimum(i, 1), 0))
SENT_ROWS = pl.BlockSpec((TILE, 768), lambda i, *info: (jnp.maximum(i - 2, 0), 0))


def kept_block(columns):
    return pl.BlockSpec(
        (TILE, columns), lambda i, info: (jnp.minimum(lax.rem(i + 2 * info[0], 4), 1), 0)
    )


def other_block(columns):
    return pl.BlockSpec(
        (TILE, columns), lambda i, info: (jnp.maximum(lax.rem(i + 2 * info[0], 4) - 2, 0), 0)
    )


def turned_block(rows):
    return pl.BlockSpec((rows, TILE), lambda i, info: (0, lax.rem(i + 2 * info[0], 4)))


PARAMS = pltpu.CompilerParams(
    vmem_limit_bytes=VMEM_LIMIT, dimension_semantics=("arbitrary",)
)


def local_forward(info, own, oth, seg_col, seg_row):
    rows = own.shape[0]
    return pl.pallas_call(
        local_forward_kernel,
        grid_spec=pltpu.PrefetchScalarGridSpec(
            num_scalar_prefetch=1,
            grid=(rows // TILE,),
            in_specs=[whole(own.shape), whole(oth.shape), whole(seg_col.shape), position_block(1)],
            out_specs=[position_block(384), position_block(8), position_block(8)],
        ),
        out_shape=[
            jax.ShapeDtypeStruct((384, rows), f32),
            jax.ShapeDtypeStruct((8, rows), f32),
            jax.ShapeDtypeStruct((8, rows), f32),
        ],
        compiler_params=PARAMS,
    )(info, own, oth, seg_col, seg_row)


def remote_forward(info, own, oth, kv, seg_col, seg_row, acc, m, l, outs):
    out_at, (first, second) = outs
    rows = own.shape[0]
    width = first.shape[0]
    return pl.pallas_call(
        functools.partial(remote_forward_kernel, out_at),
        grid_spec=pltpu.PrefetchScalarGridSpec(
            num_scalar_prefetch=1,
            grid=(rows // TILE,),
            in_specs=[
                whole(own.shape),
                whole(oth.shape),
                whole(kv.shape),
                whole(seg_col.shape),
                turned_block(1),
                turned_block(384),
                turned_block(8),
                turned_block(8),
                whole(first.shape),
                whole(second.shape),
            ],
            out_specs=[tile_of(384), turned_block(8), KEPT_ROWS, SENT_ROWS],
            scratch_shapes=[
                pltpu.VMEM((384, TILE), f32),
                pltpu.VMEM((8, TILE), f32),
                pltpu.VMEM((8, TILE), f32),
            ],
        ),
        out_shape=[
            jax.ShapeDtypeStruct((rows, 384), bf16),
            jax.ShapeDtypeStruct((8, rows), f32),
            jax.ShapeDtypeStruct((rows // 2, width), f32),
            jax.ShapeDtypeStruct((rows // 2, width), bf16),
        ],
        compiler_params=PARAMS,
    )(info, own, oth, kv, seg_col, seg_row, acc, m, l, first, second)


def backward_step(q, k, v, go, lse, delta, bias):
    p = jnp.exp(dot(k, q, ROWS_LAST) + bias - lse)
    gp = dot(v, go, ROWS_LAST)
    gs = (p * (gp - delta)).astype(bf16)
    return dot(p.astype(bf16), go, PLAIN), dot(gs, q, PLAIN), dot(k, gs, FIRST_FIRST)


def remote_backward_kernel(
    out_at,
    info_ref,
    own_ref,
    oth_ref,
    kv_ref,
    seg_col_ref,
    seg_row_ref,
    kept_ref,
    other_ref,
    first_ref,
    second_ref,
    attn_ref,
    lse_ref,
    gkv_ref,
    gq_ref,
    delta_ref,
    go_ref,
    gk_acc,
    gv_acc,
):
    i = pl.program_id(0)
    core = info_ref[0]
    query_at = physical(i, core)

    @pl.when(i == 0)
    def _():
        gk_acc[...] = jnp.zeros_like(gk_acc)
        gv_acc[...] = jnp.zeros_like(gv_acc)

    wide = rows_of(lax.rem(i + 2 * core, 4), kept_ref, other_ref)
    go_ref[:, 0:192] = dot(wide, first_ref[:, out_at[0] : out_at[0] + 192], PLAIN).astype(bf16)
    go_ref[:, 192:384] = dot(wide, second_ref[:, out_at[1] : out_at[1] + 192], PLAIN).astype(bf16)
    for pair in range(3):
        columns = slice(pair * 128, pair * 128 + 128)
        product = (go_ref[:, columns].astype(f32) * attn_ref[:, columns].astype(f32)).T
        for half in range(2):
            delta_ref[2 * pair + half : 2 * pair + half + 1, :] = jnp.sum(
                product[half * 64 : half * 64 + 64], 0, keepdims=True
            )
    delta_ref[6:8, :] = jnp.zeros((2, TILE), f32)
    gq_ref[...] = jnp.zeros_like(gq_ref)

    def step(j, carry):
        key_at = pl.multiple_of(j * REMOTE_TILE, REMOTE_TILE)
        rows = pl.ds(key_at, REMOTE_TILE)
        bias = tile_bias(seg_col_ref[rows, :], seg_row_ref[...], 0, REMOTE_ROWS)
        for h in range(6):
            ref = own_ref if h < 3 else oth_ref
            q = ref[pl.ds(query_at, TILE), head_columns(h, 0)] * bf16(0.125)
            base = (h // 3) * 384 + (h % 3) * HEAD_DIM
            k = kv_ref[rows, base : base + HEAD_DIM]
            v = kv_ref[rows, base + 192 : base + 192 + HEAD_DIM]
            go = go_ref[:, h * HEAD_DIM : (h + 1) * HEAD_DIM]
            gv, gk, gq = backward_step(
                q, k, v, go, lse_ref[h : h + 1, :], delta_ref[h : h + 1, :], bias
            )
            gv_acc[h, rows, :] += gv
            gk_acc[h, rows, :] += gk
            gq_ref[h * HEAD_DIM : (h + 1) * HEAD_DIM, :] += gq
        return carry

    lax.fori_loop(info_ref[5 + i], REMOTE_ROWS // REMOTE_TILE, step, 0)

    @pl.when(i == pl.num_programs(0) - 1)
    def _():
        for h in range(6):
            base = (h // 3) * 384 + (h % 3) * HEAD_DIM
            gkv_ref[:, base : base + HEAD_DIM] = gk_acc[h].astype(bf16)
            gkv_ref[:, base + 192 : base + 192 + HEAD_DIM] = gv_acc[h].astype(bf16)


def remote_backward(info, own, oth, kv, seg_col, seg_row, wide, outs, attn, lse):
    out_at, (first, second) = outs
    rows = own.shape[0]
    return pl.pallas_call(
        functools.partial(remote_backward_kernel, out_at),
        grid_spec=pltpu.PrefetchScalarGridSpec(
            num_scalar_prefetch=1,
            grid=(rows // TILE,),
            in_specs=[
                whole(own.shape),
                whole(oth.shape),
                whole(kv.shape),
                whole(seg_col.shape),
                position_block(1),
                kept_block(wide[0].shape[1]),
                other_block(wide[0].shape[1]),
                whole(first.shape),
                whole(second.shape),
                physical_block(384),
                position_block(8),
            ],
            out_specs=[
                whole(kv.shape), position_block(384), position_block(8), physical_block(384)
            ],
            scratch_shapes=[
                pltpu.VMEM((6, REMOTE_ROWS, HEAD_DIM), f32),
                pltpu.VMEM((6, REMOTE_ROWS, HEAD_DIM), f32),
            ],
        ),
        out_shape=[
            jax.ShapeDtypeStruct(kv.shape, bf16),
            jax.ShapeDtypeStruct((384, rows), f32),
            jax.ShapeDtypeStruct((8, rows), f32),
            jax.ShapeDtypeStruct((rows, 384), bf16),
        ],
        compiler_params=PARAMS,
    )(info, own, oth, kv, seg_col, seg_row, *wide, first, second, attn, lse)


def local_backward_kernel(
    info_ref,
    own_ref,
    oth_ref,
    seg_col_ref,
    seg_row_ref,
    go_ref,
    lse_ref,
    delta_ref,
    gq_in,
    gown_ref,
    goth_ref,
    gq_acc,
    gk_acc,
    gv_acc,
):
    i = pl.program_id(0)
    core = info_ref[0]
    query_at = physical(i, core)

    @pl.when(i == 0)
    def _():
        gk_acc[...] = jnp.zeros_like(gk_acc)
        gv_acc[...] = jnp.zeros_like(gv_acc)

    gq_acc[...] = gq_in[...]

    def step(back, carry):
        j = i - back
        rows = pl.ds(physical(j, core), TILE)
        j_pos = pl.multiple_of(j * TILE, TILE)
        bias = tile_bias(
            seg_col_ref[pl.ds(j_pos, TILE), :], seg_row_ref[...], j * TILE, i * TILE
        )
        for h in range(6):
            ref = own_ref if h < 3 else oth_ref
            q = ref[pl.ds(query_at, TILE), head_columns(h, 0)] * bf16(0.125)
            k = ref[rows, head_columns(h, 1)]
            v = ref[rows, head_columns(h, 2)]
            go = go_ref[:, h * HEAD_DIM : (h + 1) * HEAD_DIM]
            gv, gk, gq = backward_step(
                q, k, v, go, lse_ref[h : h + 1, :], delta_ref[h : h + 1, :], bias
            )
            gv_acc[h, rows, :] += gv
            gk_acc[h, rows, :] += gk
            gq_acc[h * HEAD_DIM : (h + 1) * HEAD_DIM, :] += gq
        return carry

    lax.fori_loop(0, i - info_ref[1 + i] + 1, step, 0)
    for h in range(6):
        out = gown_ref if h < 3 else goth_ref
        block = gq_acc[h * HEAD_DIM : (h + 1) * HEAD_DIM, :].T * 0.125
        out[pl.ds(query_at, TILE), head_columns(h, 0)] = block.astype(bf16)

    @pl.when(i == pl.num_programs(0) - 1)
    def _():
        for h in range(6):
            out = gown_ref if h < 3 else goth_ref
            out[:, head_columns(h, 1)] = gk_acc[h].astype(bf16)
            out[:, head_columns(h, 2)] = gv_acc[h].astype(bf16)


def local_backward(info, own, oth, seg_col, seg_row, go, lse, delta, gq):
    rows = own.shape[0]
    return pl.pallas_call(
        local_backward_kernel,
        grid_spec=pltpu.PrefetchScalarGridSpec(
            num_scalar_prefetch=1,
            grid=(rows // TILE,),
            in_specs=[
                whole(own.shape),
                whole(oth.shape),
                whole(seg_col.shape),
                position_block(1),
                physical_block(384),
                position_block(8),
                position_block(8),
                position_block(384),
            ],
            out_specs=[whole(own.shape), whole(oth.shape)],
            scratch_shapes=[
                pltpu.VMEM((384, TILE), f32),
                pltpu.VMEM((6, rows, HEAD_DIM), f32),
                pltpu.VMEM((6, rows, HEAD_DIM), f32),
            ],
        ),
        out_shape=[
            jax.ShapeDtypeStruct(own.shape, bf16),
            jax.ShapeDtypeStruct(oth.shape, bf16),
        ],
        compiler_params=PARAMS,
    )(info, own, oth, seg_col, seg_row, go, lse, delta, gq)


def normalize(v):
    center = v - jnp.mean(v, -1, keepdims=True)
    scale = lax.rsqrt(jnp.mean(center * center, -1, keepdims=True) + EPSILON)
    return center * scale, scale


def norm_forward_kernel(rounded, base_ref, part_ref, received_ref, rows_ref, total_ref, normed_ref):
    total = base_ref[...].astype(f32) + (
        part_ref[...] + received_ref[...].astype(f32) + rows_ref[0:1, :]
    )
    if rounded:
        total = total.astype(bf16)
    total_ref[...] = total
    unit, _ = normalize(total.astype(f32))
    normed_ref[...] = (unit * rows_ref[1:2, :] + rows_ref[2:3, :]).astype(bf16)


def norm_forward(base, part, received, bias, gain, shift, rounded):
    rows, width = base.shape
    vectors = jnp.stack([bias, gain, shift])
    return pl.pallas_call(
        functools.partial(norm_forward_kernel, rounded),
        grid=(rows // TILE,),
        in_specs=[tile_of(width)] * 3 + [fixed(vectors.shape)],
        out_specs=[tile_of(width)] * 2,
        out_shape=[
            jax.ShapeDtypeStruct(base.shape, bf16 if rounded else f32),
            jax.ShapeDtypeStruct(base.shape, bf16),
        ],
        compiler_params=PARAMS,
    )(base, part, received, vectors)


def norm_backward_kernel(
    v_ref, part_ref, received_ref, above_ref, gain_ref, wide_ref, low_ref, sums_ref
):
    @pl.when(pl.program_id(0) == 0)
    def _():
        sums_ref[...] = jnp.zeros_like(sums_ref)

    grad = part_ref[...] + received_ref[...].astype(f32)
    unit, scale = normalize(v_ref[...].astype(f32))
    scaled = grad * gain_ref[...]
    back = scale * (
        scaled
        - jnp.mean(scaled, -1, keepdims=True)
        - unit * jnp.mean(scaled * unit, -1, keepdims=True)
    )
    total = above_ref[...].astype(f32) + back
    wide_ref[...] = total
    low = total.astype(bf16)
    low_ref[...] = low
    sums_ref[0:1, :] += jnp.sum(grad * unit, 0, keepdims=True)
    sums_ref[1:2, :] += jnp.sum(grad, 0, keepdims=True)
    sums_ref[2:3, :] += jnp.sum(low.astype(f32), 0, keepdims=True)


def norm_backward(v, part, received, above, gain):
    rows, width = v.shape
    return pl.pallas_call(
        norm_backward_kernel,
        grid=(rows // TILE,),
        in_specs=[tile_of(width)] * 4 + [fixed((1, width))],
        out_specs=[tile_of(width)] * 2 + [fixed((8, width))],
        out_shape=[
            jax.ShapeDtypeStruct(v.shape, f32),
            jax.ShapeDtypeStruct(v.shape, bf16),
            jax.ShapeDtypeStruct((8, width), f32),
        ],
        compiler_params=PARAMS,
    )(v, part, received, above, gain[None])


def both_rows(own):
    return jnp.concatenate([own, swap_core(own)], 0)


def split_sum(parts):
    half = parts[0][0].shape[0] // 2

    def partial(rows):
        return sum(dot(a[rows], b, ROWS_LAST) for a, b in parts)

    received = swap_core(partial(slice(half, None)).astype(bf16))
    return partial(slice(0, half)), received


def gelu_and_slope(v):
    c, a = 0.7978845608028654, 0.044715
    square = v * v
    t = jnp.tanh(c * v * (1.0 + a * square))
    half = 0.5 * (1.0 + t)
    slope = half + 0.5 * v * (1.0 - t * t) * (c * (1.0 + 3.0 * a * square))
    return v * half, slope


def units_forward_kernel(widths, kept_ref, other_ref, *refs):
    count = len(widths)
    ups, downs = refs[:count], refs[count : 2 * count]
    bias_ref, hidden_ref, slope_ref, part_ref, sent_ref = refs[2 * count :]
    x = rows_of(pl.program_id(0), kept_ref, other_ref)
    at, total = 0, None
    for width, up, down in zip(widths, ups, downs):
        columns = slice(at, at + width)
        value, slope = gelu_and_slope(dot(x, up[:, :width], PLAIN) + bias_ref[:, columns])
        value = value.astype(bf16)
        hidden_ref[:, columns] = value
        slope_ref[:, columns] = slope.astype(bf16)
        term = dot(value, down[...], ROWS_LAST)
        total = term if total is None else total + term
        at += width
    store_rows(pl.program_id(0), total, part_ref, sent_ref)


def units_forward(x, ups, downs, bias):
    rows, width = 2 * x[0].shape[0], x[0].shape[1]
    widths = [w.shape[1] for w in downs]
    units = sum(widths)
    return pl.pallas_call(
        functools.partial(units_forward_kernel, widths),
        grid=(rows // TILE,),
        in_specs=[KEPT_ROWS, SENT_ROWS]
        + [fixed(w.shape) for w in ups + downs]
        + [fixed((1, units))],
        out_specs=[tile_of(units), tile_of(units), KEPT_ROWS, SENT_ROWS],
        out_shape=[
            jax.ShapeDtypeStruct((rows, units), bf16),
            jax.ShapeDtypeStruct((rows, units), bf16),
            jax.ShapeDtypeStruct((rows // 2, width), f32),
            jax.ShapeDtypeStruct((rows // 2, width), bf16),
        ],
        compiler_params=PARAMS,
    )(*x, *ups, *downs, bias[None])


def units_backward_kernel(widths, kept_ref, other_ref, slope_ref, *refs):
    count = len(widths)
    ups, downs = refs[:count], refs[count : 2 * count]
    gpre_ref, part_ref, sent_ref, sums_ref = refs[2 * count :]

    @pl.when(pl.program_id(0) == 0)
    def _():
        sums_ref[...] = jnp.zeros_like(sums_ref)

    g = rows_of(pl.program_id(0), kept_ref, other_ref)
    at, total = 0, None
    for width, up, down in zip(widths, ups, downs):
        columns = slice(at, at + width)
        gpre = (dot(g, down[...], PLAIN) * slope_ref[:, columns].astype(f32)).astype(bf16)
        gpre_ref[:, columns] = gpre
        sums_ref[0:1, columns] += jnp.sum(gpre.astype(f32), 0, keepdims=True)
        term = dot(gpre, up[:, :width], ROWS_LAST)
        total = term if total is None else total + term
        at += width
    store_rows(pl.program_id(0), total, part_ref, sent_ref)


def units_backward(g, slopes, ups, downs):
    rows, width = 2 * g[0].shape[0], g[0].shape[1]
    units = slopes.shape[1]
    return pl.pallas_call(
        functools.partial(units_backward_kernel, [w.shape[1] for w in downs]),
        grid=(rows // TILE,),
        in_specs=[KEPT_ROWS, SENT_ROWS, tile_of(units)] + [fixed(w.shape) for w in ups + downs],
        out_specs=[tile_of(units), KEPT_ROWS, SENT_ROWS, fixed((8, units))],
        out_shape=[
            jax.ShapeDtypeStruct((rows, units), bf16),
            jax.ShapeDtypeStruct((rows // 2, width), f32),
            jax.ShapeDtypeStruct((rows // 2, width), bf16),
            jax.ShapeDtypeStruct((8, units), f32),
        ],
        compiler_params=PARAMS,
    )(*g, slopes, *ups, *downs)


def block_forward(h, normed, masks, weights, vectors, hook):
    info, seg_col, seg_row, seg_far_col, is_first_core = masks
    qkv, outs, up, down = weights
    _, _, out_bias, ln2_gain, ln2_shift, _, qkv_bias, up_bias = vectors
    normed = both_rows(hook(K.ROWS, normed))
    proj = [(dot(normed, qkv[n], PLAIN) + qkv_bias[n]).astype(bf16) for n in range(2)]
    half = normed.shape[0] // 2
    keys = jnp.concatenate([proj[1][:, 192:], proj[0][:, 192:]], 1)
    early = jnp.where(is_first_core, keys[:half], keys[half:])
    late = jnp.where(is_first_core, keys[half:], keys[:half])
    sent = jnp.concatenate([early[half - (REMOTE_ROWS - half) :], late], 0)
    far = lax.ppermute(hook(K.SENT, sent), TENSOR, [(0, 2), (1, 3)])
    proj = hook(K.ATTEND, proj)
    state = local_forward(info, proj[0], proj[1], seg_col, seg_row)
    far = hook(K.FAR, far)
    attn, lse, part, sent = remote_forward(
        info, proj[0], proj[1], far, seg_far_col, seg_row, *state, outs
    )
    received = hook(K.MIDDLE, swap_core(sent))
    middle, second = norm_forward(h, part, received, out_bias, ln2_gain, ln2_shift, False)
    second = hook(K.SECOND, [second, swap_core(second)])
    hidden, slopes, part, sent = units_forward(second, up, down, jnp.concatenate(up_bias))
    received = hook(K.HIDDEN, swap_core(sent))
    return (middle, part, received), (h, middle, normed, proj, far, attn, lse, second, hidden, slopes)


def block_backward(gy, masks, saved, weights, vectors, grads, hook):
    info, seg_col, seg_row, seg_far_col, is_first_core = masks
    qkv, outs, up, down = weights
    ln1_gain, ln2_gain = vectors[0], vectors[3]
    h, middle, normed, proj, far, attn, lse, second, hidden, slopes = saved
    wide = [gy, swap_core(gy)]
    gpre, part, sent, up_sums = units_backward(wide, slopes, up, down)
    wide, second = jnp.concatenate(wide, 0), jnp.concatenate(second, 0)
    grads[K.GPRE] = sent
    received = swap_core(sent)
    units = hidden.shape[1] // 2
    g_down = dot(wide, hidden, FIRST_FIRST).astype(bf16)
    g_up = dot(second, gpre, FIRST_FIRST).astype(bf16)
    grads[K.DOWN] = [g_down[:, :units], g_down[:, units:]]
    grads[K.UP] = [g_up[:, :units], g_up[:, units:]]
    received = hook(K.GPRE, after(received, g_down, g_up))
    gmid, gmr, sums2 = norm_backward(middle, part, received, gy, ln2_gain)
    mid_wide = hook(K.GMR, [gmr, swap_core(gmr)])
    gfar, gq, delta, gattn = remote_backward(
        info, proj[0], proj[1], far, seg_far_col, seg_row, mid_wide, outs, attn, lse
    )
    gnear = lax.ppermute(gfar, TENSOR, [(2, 0), (3, 1)])
    mid_wide = jnp.concatenate(mid_wide, 0)
    grads[K.OUT] = [
        dot(mid_wide, attn[:, n * 192 : n * 192 + 192], FIRST_FIRST).astype(bf16) for n in range(2)
    ]
    gproj = local_backward(info, proj[0], proj[1], seg_col, seg_row, gattn, lse, delta, gq)
    grads[K.GPROJ] = gproj[0]
    gproj = hook(K.GPROJ, gproj)
    half = normed.shape[0] // 2
    gnear = jnp.pad(gnear, ((2 * half - REMOTE_ROWS, 0), (0, 0)))
    gnear = jnp.concatenate(
        [
            jnp.where(is_first_core, gnear[:half], gnear[half:]),
            jnp.where(is_first_core, gnear[half:], gnear[:half]),
        ],
        0,
    )
    gproj = [
        (gproj[n].astype(f32) + jnp.pad(gnear[:, at : at + 384].astype(f32), ((0, 0), (192, 0))))
        .astype(bf16)
        for n, at in ((0, 384), (1, 0))
    ]
    g_qkv_bias = [jnp.sum(g.astype(f32), 0) for g in gproj]
    grads[K.QKV] = [dot(normed, gproj[n], FIRST_FIRST).astype(bf16) for n in range(2)]
    grads[K.MARK] = grads[K.QKV][1]
    part, received = split_sum([(gproj[0], qkv[0]), (gproj[1], qkv[1])])
    received = hook(K.GNORMED, received)
    _, gin, sums1 = norm_backward(h, part, received, gmid, ln1_gain)
    rows_grads = [sums1[0], sums1[1], sums2[2], sums2[0], sums2[1]]
    g_up_bias = [up_sums[0, :units], up_sums[0, units:]]
    return gin, rows_grads, sums1[2], (g_qkv_bias, g_up_bias)


class Stages:
    def __init__(self):
        self.makers, self.made = {}, {}

    def __getitem__(self, key):
        if key not in self.made:
            self.made[key] = self.makers[key]()
        return self.made[key]

    def hook(self, plan):
        def tie(name, value):
            keys = plan.get(name, ())
            return after(value, *[self[key] for key in keys]) if keys else value

        return tie


def section_first(v, is_leading):
    half = v.shape[-1] // 2
    return jnp.where(is_leading, v, jnp.concatenate([v[..., half:], v[..., :half]], -1))


def body(
    tokens,
    segments,
    cotangent,
    ln1_gain,
    ln1_shift,
    qkv_weight,
    qv_bias,
    out_weight,
    out_bias,
    ln2_gain,
    ln2_shift,
    up_weight,
    up_bias,
    down_weight,
    down_bias,
):
    section = lax.axis_index(SECTION)
    is_leading = section == 0
    tensor = lax.axis_index(TENSOR)
    core = lax.rem(tensor, 2)
    chip = tensor // 2
    dp = lax.axis_index(DP)
    dp_size = lax.axis_size(DP)
    place = dp.astype(jnp.int32).reshape(1)
    share = ln1_gain.shape[1]
    features = share * dp_size
    local_width = qkv_weight.shape[3]
    local_units = up_weight.shape[2]

    row = jnp.concatenate(
        [
            ln1_gain[0],
            ln1_shift[0],
            out_bias[0],
            ln2_gain[0],
            ln2_shift[0],
            down_bias[0],
            qv_bias[0].reshape(-1),
            up_bias[0].reshape(-1),
        ]
    )[None]
    other_row = swap_section(row)
    rows = jnp.where(
        is_leading, jnp.concatenate([row, other_row], 1), jnp.concatenate([other_row, row], 1)
    )
    rows = jnp.concatenate([rows, swap_chip(rows)], 1)
    if dp_size == 4:
        pieces = [rows] + [shift_dp(rows, k) for k in range(1, dp_size)]
        rows = jnp.zeros((dp_size,) + rows.shape[1:], rows.dtype)
        for k in range(dp_size):
            rows = lax.dynamic_update_slice_in_dim(
                rows, pieces[k], lax.rem(dp + dp_size - k, dp_size), 0
            )
    else:
        rows = lax.all_gather(rows, DP, axis=0, tiled=True)
    length = row.shape[1]
    rows = rows.reshape(dp_size, 2, 2, length).astype(f32)
    qv_share = local_width // dp_size
    up_share = local_units // dp_size

    def vectors_of(b):
        plain = [rows[:, 0, b, n * share : (n + 1) * share].reshape(-1) for n in range(6)]
        qkv_bias, up_biases = [], []
        for n in range(2):
            at = 6 * share
            query = rows[:, n, b, at : at + qv_share].reshape(-1)
            value = rows[:, n, b, at + qv_share : at + 2 * qv_share].reshape(-1)
            qkv_bias.append(jnp.concatenate([query, jnp.zeros_like(query), value]))
            up_biases.append(rows[:, n, b, at + 2 * qv_share :].reshape(-1))
        up_biases[1] = section_first(up_biases[1], is_leading)
        return tuple(plain) + (qkv_bias, up_biases)

    vectors = [vectors_of(b) for b in range(2)]

    qkv_columns = 3 * local_width
    out_at = -(-qkv_columns // 128) * 128
    stages = Stages()
    first_slab = jnp.concatenate(
        [
            qkv_weight[0].reshape(share, qkv_columns),
            jnp.zeros((share, out_at - qkv_columns), bf16),
            out_weight[0].T,
        ],
        1,
    )
    slabs = {K.FIRST: first_slab, K.UP: up_weight[0], K.DOWN: down_weight[0].T}
    others = {K.FIRST: swap_section(first_slab)}
    for name in (K.UP, K.DOWN):
        others[name] = swap_section(after(slabs[name], others[K.FIRST]))

    def describe(b, name):
        def pick():
            return jnp.where(section == b, slabs[name], others[name])

        stages.makers[K.PICK, b, name] = pick
        stages.makers[K.DP, b, name] = lambda: gather_dp(stages[K.PICK, b, name])
        if name == K.FIRST:
            stages.makers[K.CHIP, b, name] = lambda: swap_chip(stages[K.DP, b, name])
            return
        half = local_units // 2

        def my_half():
            full = stages[K.DP, b, name]
            return jnp.where(is_leading, full[:, :half], full[:, half:])

        stages.makers[K.CHIP, b, name] = lambda: swap_chip(my_half())
        stages.makers[K.SECTION, b, name] = lambda: swap_section(stages[K.CHIP, b, name])
        stages.makers[K.ALL, b, name] = lambda: [
            stages[K.DP, b, name], stages[K.CHIP, b, name], stages[K.SECTION, b, name]
        ]

    for b in range(2):
        for name in slabs:
            describe(b, name)

    def weights_of(b):
        first = [stages[K.DP, b, K.FIRST], stages[K.CHIP, b, K.FIRST]]
        return (
            [w[:, :qkv_columns] for w in first],
            ((out_at, out_at), first),
            stages[K.ALL, b, K.UP],
            stages[K.ALL, b, K.DOWN],
        )

    seg = jnp.where(is_leading, segments[0, 0], segments[1, 0])
    near_len = seg.shape[0] // 2
    seg_near = lax.dynamic_slice_in_dim(seg, chip * near_len, near_len, 0)
    seg_far = seg[near_len - REMOTE_ROWS : near_len]
    heads_of = seg_near[::TILE]
    start = jnp.sum((seg_near[None, :] < heads_of[:, None]).astype(jnp.int32), 1)
    far_start = jnp.sum((seg_far < seg_far[-1]).astype(jnp.int32))
    crosses = (heads_of == seg_far[-1]) & (chip == 1)
    info = jnp.concatenate(
        [
            core.astype(jnp.int32).reshape(1),
            start // TILE,
            jnp.where(crosses, far_start // REMOTE_TILE, REMOTE_ROWS // REMOTE_TILE),
        ]
    ).astype(jnp.int32)
    masks = (info, seg_near[:, None], seg_near[None, :], seg_far[:, None], core == 0)

    h = jnp.where(is_leading, tokens[0, 0], tokens[1, 0])
    normed = normalize(h.astype(f32))[0] * vectors[0][0] + vectors[0][1]
    normed = normed.astype(bf16)
    outs, saved, weights, back = [], [], [], [None, None]
    stages.makers[K.OUT, 0] = lambda: lax.ppermute(outs[0], SECTION, [(1, 0)])
    stages.makers[K.OUT, 1] = lambda: lax.ppermute(outs[1], SECTION, [(0, 1)])
    stages.makers[K.BACK, 1] = lambda: lax.ppermute(back[1], SECTION, [(0, 1)])
    stages.makers[K.BACK, 0] = lambda: lax.ppermute(back[0], SECTION, [(1, 0)])
    plans = (
        {
            K.ATTEND: ((K.DP, 0, K.UP), (K.PICK, 0, K.DOWN)),
            K.FAR: ((K.CHIP, 0, K.UP), (K.DP, 0, K.DOWN)),
            K.MIDDLE: ((K.SECTION, 0, K.UP), (K.DP, 1, K.FIRST)),
            K.SECOND: ((K.CHIP, 0, K.DOWN), (K.DP, 1, K.UP)),
            K.HIDDEN: ((K.CHIP, 1, K.FIRST),),
        },
        {
            K.SENT: ((K.CHIP, 1, K.UP),),
            K.FAR: ((K.SECTION, 1, K.UP), (K.DP, 1, K.DOWN)),
            K.MIDDLE: ((K.CHIP, 1, K.DOWN), (K.OUT, 0)),
        },
    )
    for b in range(2):
        weights.append(weights_of(b))
        (middle, part, received), kept = block_forward(
            h, normed, masks, weights[b], vectors[b], stages.hook(plans[b])
        )
        saved.append(kept)
        bias = vectors[b][5]
        if b == 0:
            h, normed = norm_forward(
                middle, part, received, bias, vectors[1][0], vectors[1][1], True
            )
            outs.append(h)
        else:
            outs.append((middle + (part + received.astype(f32) + bias)).astype(bf16))

    gy = jnp.where(is_leading, cotangent[0, 0], cotangent[1, 0])
    above_sum = jnp.sum(gy.astype(f32), 0)
    row_grads = [None, None]
    unit_grads = [None, None]
    grads = [{}, {}]

    def not_before(b, received):
        return after(received, grads[0][K.GPRE]) if b == 1 else received

    def halves(v):
        return v[:, : v.shape[1] // 2], v[:, v.shape[1] // 2 :]

    def describe_back(b):
        parts = (K.DOWN, K.UP)

        def section_half():
            theirs, others = [], []
            for name in parts:
                own, other = grads[b][name]
                low, high = halves(own)
                theirs.append(jnp.where(is_leading, high, low))
                others.append(halves(other)[1])
            received = swap_section(jnp.concatenate(theirs + others, 1))
            return after(received, grads[0][K.GPROJ]) if b == 0 else received

        def chip_half():
            mine = jnp.concatenate([halves(grads[b][name][1])[0] for name in parts], 1)
            received = after(stages[K.GSECTION, b], grads[b][K.MARK])
            total = mine.astype(f32) + halves(received)[1].astype(f32)
            return not_before(b, swap_chip(total.astype(bf16)))

        def units():
            mine = []
            for name in parts:
                low, high = halves(grads[b][name][0])
                mine.append(jnp.where(is_leading, low, high))
            total = jnp.concatenate(mine, 1).astype(f32)
            total = total + halves(stages[K.GSECTION, b])[0].astype(f32)
            total = total + stages[K.GCHIP, b, K.UNITS].astype(f32)
            return total.astype(bf16)

        def joined(n):
            return jnp.concatenate([grads[b][K.OUT][n], grads[b][K.QKV][n]], 1)

        def heads():
            total = joined(0).astype(f32) + stages[K.GCHIP, b, K.HEADS].astype(f32)
            return total.astype(bf16)

        stages.makers[K.GSECTION, b] = section_half
        stages.makers[K.GCHIP, b, K.UNITS] = chip_half
        stages.makers[K.GCHIP, b, K.HEADS] = lambda: not_before(b, swap_chip(joined(1)))
        stages.makers[K.PICK, b, K.UNITS] = units
        stages.makers[K.PICK, b, K.HEADS] = heads
        stages.makers[K.GDP, b, K.UNITS] = lambda: scatter_dp(stages[K.PICK, b, K.UNITS])
        stages.makers[K.GDP, b, K.HEADS] = lambda: scatter_dp(stages[K.PICK, b, K.HEADS])

    for b in range(2):
        describe_back(b)
    plans = (
        {
            K.GPRE: ((K.GCHIP, 1, K.HEADS), (K.OUT, 1)),
            K.GMR: ((K.GCHIP, 1, K.UNITS),),
            K.GPROJ: ((K.GSECTION, 0), (K.GDP, 1, K.HEADS)),
            K.GNORMED: ((K.GCHIP, 0, K.UNITS), (K.GDP, 1, K.UNITS), (K.BACK, 1)),
        },
        {
            K.GNORMED: (),
        },
    )
    for b in (1, 0):
        gy, plain_grads, below_sum, unit_grads[b] = block_backward(
            gy, masks, saved[b], weights[b], vectors[b], grads[b], stages.hook(plans[b])
        )
        back[b] = gy
        row_grads[b] = plain_grads + [above_sum]
        above_sum = below_sum

    pair = stages[K.GDP, 0, K.HEADS], stages[K.GDP, 1, K.HEADS]
    keep = jnp.where(is_leading, pair[0], pair[1])
    give = jnp.where(is_leading, pair[1], pair[0])
    g_heads = keep.astype(f32) + swap_section(give).astype(f32)
    g_out, g_qkv = g_heads[:, :local_width], g_heads[:, local_width:]
    pair = stages[K.GDP, 0, K.UNITS], stages[K.GDP, 1, K.UNITS]
    keep = jnp.where(is_leading, pair[0], pair[1])
    give = jnp.where(is_leading, pair[1], pair[0])
    keep, other = keep.astype(f32), swap_section(give).astype(f32)
    half = local_units // 2

    def in_order(at):
        mine, theirs = keep[:, at : at + half], other[:, at : at + half]
        return jnp.concatenate(
            [jnp.where(is_leading, mine, theirs), jnp.where(is_leading, theirs, mine)], 1
        )

    g_down, g_up = in_order(0), in_order(half)

    plain = jnp.stack([jnp.concatenate(row_grads[b]) for b in range(2)])
    plain = after(plain, stages[K.PICK, 0, K.UNITS])
    plain = plain + swap_core(plain)
    units = [
        jnp.stack(
            [
                jnp.concatenate(
                    [
                        unit_grads[b][0][n],
                        unit_grads[b][1][n]
                        if n == 0
                        else section_first(unit_grads[b][1][n], is_leading),
                    ]
                )
                for b in range(2)
            ]
        )
        for n in range(2)
    ]
    swapped = swap_chip(jnp.concatenate([plain, units[1]], 1))
    plain_width = plain.shape[1]
    total = jnp.concatenate([plain, units[0]], 1) + swapped
    total = after(total, stages[K.PICK, 0, K.HEADS])
    total = total_dp(total)
    keep = jnp.where(is_leading, total[0], total[1])
    give = jnp.where(is_leading, total[1], total[0])
    total = keep + swap_section(give[None])[0]

    def mine(vector):
        part = vector.shape[0] // dp_size
        return lax.dynamic_slice_in_dim(vector, dp * part, part, 0)

    shares = [mine(total[n * features : (n + 1) * features]) for n in range(6)]
    unit_total = total[plain_width:]
    g_query = mine(unit_total[:local_width])
    g_value = mine(unit_total[2 * local_width : 3 * local_width])
    g_up_bias = mine(unit_total[3 * local_width :])

    def exchanged(name, pair):
        own = jnp.where(is_leading, pair[0], pair[1])
        other = jnp.where(is_leading, stages[name, 0], stages[name, 1])
        return jnp.stack(
            [jnp.where(is_leading, own, other), jnp.where(is_leading, other, own)]
        )[None, :, None]

    return (
        exchanged(K.OUT, outs),
        exchanged(K.BACK, back),
        shares[0][None],
        shares[1][None],
        g_qkv.reshape(1, share, 3, local_width),
        jnp.stack([g_query, g_value])[None, :, None],
        g_out.T[None],
        shares[2][None],
        shares[3][None],
        shares[4][None],
        g_up[None],
        g_up_bias[None, None],
        g_down.T[None],
        shares[5][None],
    )


def solution(mesh):
    placed = (
        P(None, DP, TENSOR, None),
        P(None, DP, None),
        P(None, DP, TENSOR, None),
        P(SECTION, DP),
        P(SECTION, DP),
        P(SECTION, DP, None, TENSOR),
        P(SECTION, None, TENSOR, DP),
        P(SECTION, TENSOR, DP),
        P(SECTION, DP),
        P(SECTION, DP),
        P(SECTION, DP),
        P(SECTION, DP, TENSOR),
        P(SECTION, TENSOR, DP),
        P(SECTION, TENSOR, DP),
        P(SECTION, DP),
    )
    return jax.shard_map(
        body,
        mesh=mesh,
        in_specs=placed,
        out_specs=(
            P(SECTION, None, DP, TENSOR, None),
            P(SECTION, None, DP, TENSOR, None),
            P(SECTION, DP),
            P(SECTION, DP),
            P(SECTION, DP, None, TENSOR),
            P(SECTION, None, TENSOR, DP),
            P(SECTION, TENSOR, DP),
            P(SECTION, DP),
            P(SECTION, DP),
            P(SECTION, DP),
            P(SECTION, DP, TENSOR),
            P(SECTION, TENSOR, DP),
            P(SECTION, TENSOR, DP),
            P(SECTION, DP),
        ),
        check_vma=False,
    )
```

```python
import functools

import jax
import jax.numpy as jnp
from jax import lax
from jax.experimental import pallas as pl
from jax.experimental.pallas import tpu as pltpu
from jax.sharding import PartitionSpec as P

HEAD_DIM = 64
DOC_MOST = 800
EPSILON = 1e-05
TILE = 256
REMOTE_TILE = 160
REMOTE_ROWS = 800
MASKED = -1e30
VMEM_LIMIT = 48 * 1024 * 1024

CORE_SWAP = [(0, 1), (1, 0), (2, 3), (3, 2)]
CHIP_SWAP = [(0, 2), (2, 0), (1, 3), (3, 1)]
SECTION_SWAP = [(0, 1), (1, 0)]

f32 = jnp.float32
bf16 = jnp.bfloat16


SECTION, DP, TENSOR = "section", "dp", "tensor"


class K:
    (
        ROWS,
        SENT,
        ATTEND,
        FAR,
        MIDDLE,
        SECOND,
        HIDDEN,
        GPRE,
        DOWN,
        UP,
        GMR,
        OUT,
        GPROJ,
        QKV,
        MARK,
        GNORMED,
        FIRST,
        PICK,
        DP,
        CHIP,
        SECTION,
        ALL,
        BACK,
        GSECTION,
        GCHIP,
        UNITS,
        HEADS,
        GDP,
    ) = range(28)


def swap_core(v):
    return lax.ppermute(v, TENSOR, CORE_SWAP)


def swap_chip(v):
    return lax.ppermute(v, TENSOR, CHIP_SWAP)


def swap_section(v):
    return lax.ppermute(v, SECTION, SECTION_SWAP)


def shift_dp(v, by):
    n = lax.axis_size(DP)
    return lax.ppermute(v, DP, [(i, (i + by) % n) for i in range(n)])


def gather_dp(v):
    return lax.all_gather(v, DP, axis=0, tiled=True)


def scatter_dp(v):
    return lax.psum_scatter(v, DP, scatter_dimension=0, tiled=True)


def total_dp(v):
    n = lax.axis_size(DP)
    if n != 4:
        return lax.psum(v, DP)
    return v + shift_dp(v, 1) + shift_dp(v, 2) + shift_dp(v, 3)


def after(value, *others):
    return lax.optimization_barrier((value, others))[0]


def dot(a, b, dims):
    return lax.dot_general(a, b, (dims, ((), ())), preferred_element_type=f32)


ROWS_LAST = ((1,), (1,))
FIRST_FIRST = ((0,), (0,))
PLAIN = ((1,), (0,))


def tile_bias(seg_keys, seg_queries, key_at, query_at):
    shape = (seg_keys.shape[0], seg_queries.shape[1])
    key_pos = lax.broadcasted_iota(jnp.int32, shape, 0) + key_at
    query_pos = lax.broadcasted_iota(jnp.int32, shape, 1) + query_at
    allowed = (seg_keys == seg_queries) & (key_pos <= query_pos)
    return jnp.where(allowed, 0.0, MASKED).astype(f32)


def physical(tile, core):
    return pl.multiple_of(lax.rem(tile + 2 * core, 4) * TILE, TILE)


def head_columns(h, kind):
    at = kind * 192 + (h % 3) * HEAD_DIM
    return slice(at, at + HEAD_DIM)


def online_step(h, s, v, m_ref, l_ref, acc_ref):
    m_old = m_ref[h : h + 1, :]
    m_new = jnp.maximum(m_old, jnp.max(s, 0, keepdims=True))
    p = jnp.exp(s - m_new)
    alpha = jnp.exp(m_old - m_new)
    m_ref[h : h + 1, :] = m_new
    l_ref[h : h + 1, :] = l_ref[h : h + 1, :] * alpha + jnp.sum(p, 0, keepdims=True)
    rows = slice(h * HEAD_DIM, (h + 1) * HEAD_DIM)
    acc_ref[rows, :] = acc_ref[rows, :] * alpha + dot(v, p.astype(bf16), FIRST_FIRST)


def local_forward_kernel(
    info_ref, own_ref, oth_ref, seg_col_ref, seg_row_ref, acc_ref, m_ref, l_ref
):
    i = pl.program_id(0)
    core = info_ref[0]
    query_at = physical(i, core)
    m_ref[...] = jnp.full_like(m_ref, MASKED)
    l_ref[...] = jnp.zeros_like(l_ref)
    acc_ref[...] = jnp.zeros_like(acc_ref)

    def step(back, carry):
        j = i - back
        key_at = physical(j, core)
        j_pos = pl.multiple_of(j * TILE, TILE)
        bias = tile_bias(
            seg_col_ref[pl.ds(j_pos, TILE), :], seg_row_ref[...], j * TILE, i * TILE
        )
        for h in range(6):
            ref = own_ref if h < 3 else oth_ref
            q = ref[pl.ds(query_at, TILE), head_columns(h, 0)] * bf16(0.125)
            k = ref[pl.ds(key_at, TILE), head_columns(h, 1)]
            v = ref[pl.ds(key_at, TILE), head_columns(h, 2)]
            online_step(h, dot(k, q, ROWS_LAST) + bias, v, m_ref, l_ref, acc_ref)
        return carry

    lax.fori_loop(0, i - info_ref[1 + i] + 1, step, 0)


def remote_forward_kernel(
    out_at,
    info_ref,
    own_ref,
    oth_ref,
    kv_ref,
    seg_col_ref,
    seg_row_ref,
    acc_in,
    m_in,
    l_in,
    first_ref,
    second_ref,
    attn_ref,
    lse_ref,
    part_ref,
    sent_ref,
    acc_ref,
    m_ref,
    l_ref,
):
    block = pl.program_id(0)
    i = lax.rem(block + 2 * info_ref[0], 4)
    query_at = pl.multiple_of(block * TILE, TILE)
    m_ref[...] = m_in[...]
    l_ref[...] = l_in[...]
    acc_ref[...] = acc_in[...]

    def step(j, carry):
        key_at = pl.multiple_of(j * REMOTE_TILE, REMOTE_TILE)
        bias = tile_bias(
            seg_col_ref[pl.ds(key_at, REMOTE_TILE), :], seg_row_ref[...], 0, REMOTE_ROWS
        )
        for h in range(6):
            ref = own_ref if h < 3 else oth_ref
            q = ref[pl.ds(query_at, TILE), head_columns(h, 0)] * bf16(0.125)
            base = (h // 3) * 384 + (h % 3) * HEAD_DIM
            k = kv_ref[pl.ds(key_at, REMOTE_TILE), base : base + HEAD_DIM]
            v = kv_ref[pl.ds(key_at, REMOTE_TILE), base + 192 : base + 192 + HEAD_DIM]
            online_step(h, dot(k, q, ROWS_LAST) + bias, v, m_ref, l_ref, acc_ref)
        return carry

    lax.fori_loop(info_ref[5 + i], REMOTE_ROWS // REMOTE_TILE, step, 0)
    l = l_ref[0:6, :]
    lse_ref[0:6, :] = m_ref[0:6, :] + jnp.log(l)
    lse_ref[6:8, :] = jnp.zeros((2, TILE), f32)
    inverse = 1.0 / l
    for pair in range(3):
        rows = slice(pair * 128, pair * 128 + 128)
        top = acc_ref[pair * 128 : pair * 128 + 64, :] * inverse[2 * pair : 2 * pair + 1, :]
        low = acc_ref[pair * 128 + 64 : pair * 128 + 128, :] * inverse[2 * pair + 1 : 2 * pair + 2, :]
        attn_ref[:, rows] = jnp.concatenate([top, low], 0).T.astype(bf16)
    total = dot(attn_ref[:, 0:192], first_ref[:, out_at[0] : out_at[0] + 192], ROWS_LAST)
    total += dot(attn_ref[:, 192:384], second_ref[:, out_at[1] : out_at[1] + 192], ROWS_LAST)
    store_rows(block, total, part_ref, sent_ref)


def rows_of(block, kept_ref, other_ref):
    return jnp.where(block < 2, kept_ref[...], other_ref[...])


def store_rows(block, total, part_ref, sent_ref):
    half = pl.num_programs(0) // 2

    @pl.when(block < half)
    def _():
        part_ref[...] = total

    @pl.when(block >= half)
    def _():
        sent_ref[...] = total.astype(bf16)


def whole(shape):
    return pl.BlockSpec(shape, lambda i, info: (0,) * len(shape))


def position_block(rows):
    return pl.BlockSpec((rows, TILE), lambda i, info: (0, i))


def physical_block(columns):
    return pl.BlockSpec((TILE, columns), lambda i, info: (lax.rem(i + 2 * info[0], 4), 0))


def tile_of(columns):
    return pl.BlockSpec((TILE, columns), lambda i, *info: (i, 0))


def fixed(shape):
    return pl.BlockSpec(shape, lambda i, *info: (0,) * len(shape))


KEPT_ROWS = pl.BlockSpec((TILE, 768), lambda i, *info: (jnp.minimum(i, 1), 0))
SENT_ROWS = pl.BlockSpec((TILE, 768), lambda i, *info: (jnp.maximum(i - 2, 0), 0))


def kept_block(columns):
    return pl.BlockSpec(
        (TILE, columns), lambda i, info: (jnp.minimum(lax.rem(i + 2 * info[0], 4), 1), 0)
    )


def other_block(columns):
    return pl.BlockSpec(
        (TILE, columns), lambda i, info: (jnp.maximum(lax.rem(i + 2 * info[0], 4) - 2, 0), 0)
    )


def turned_block(rows):
    return pl.BlockSpec((rows, TILE), lambda i, info: (0, lax.rem(i + 2 * info[0], 4)))


PARAMS = pltpu.CompilerParams(
    vmem_limit_bytes=VMEM_LIMIT, dimension_semantics=("arbitrary",)
)


def local_forward(info, own, oth, seg_col, seg_row):
    rows = own.shape[0]
    return pl.pallas_call(
        local_forward_kernel,
        grid_spec=pltpu.PrefetchScalarGridSpec(
            num_scalar_prefetch=1,
            grid=(rows // TILE,),
            in_specs=[whole(own.shape), whole(oth.shape), whole(seg_col.shape), position_block(1)],
            out_specs=[position_block(384), position_block(8), position_block(8)],
        ),
        out_shape=[
            jax.ShapeDtypeStruct((384, rows), f32),
            jax.ShapeDtypeStruct((8, rows), f32),
            jax.ShapeDtypeStruct((8, rows), f32),
        ],
        compiler_params=PARAMS,
    )(info, own, oth, seg_col, seg_row)


def remote_forward(info, own, oth, kv, seg_col, seg_row, acc, m, l, outs):
    out_at, (first, second) = outs
    rows = own.shape[0]
    width = first.shape[0]
    return pl.pallas_call(
        functools.partial(remote_forward_kernel, out_at),
        grid_spec=pltpu.PrefetchScalarGridSpec(
            num_scalar_prefetch=1,
            grid=(rows // TILE,),
            in_specs=[
                whole(own.shape),
                whole(oth.shape),
                whole(kv.shape),
                whole(seg_col.shape),
                turned_block(1),
                turned_block(384),
                turned_block(8),
                turned_block(8),
                whole(first.shape),
                whole(second.shape),
            ],
            out_specs=[tile_of(384), turned_block(8), KEPT_ROWS, SENT_ROWS],
            scratch_shapes=[
                pltpu.VMEM((384, TILE), f32),
                pltpu.VMEM((8, TILE), f32),
                pltpu.VMEM((8, TILE), f32),
            ],
        ),
        out_shape=[
            jax.ShapeDtypeStruct((rows, 384), bf16),
            jax.ShapeDtypeStruct((8, rows), f32),
            jax.ShapeDtypeStruct((rows // 2, width), f32),
            jax.ShapeDtypeStruct((rows // 2, width), bf16),
        ],
        compiler_params=PARAMS,
    )(info, own, oth, kv, seg_col, seg_row, acc, m, l, first, second)


def backward_step(q, k, v, go, lse, delta, bias):
    p = jnp.exp(dot(k, q, ROWS_LAST) + bias - lse)
    gp = dot(v, go, ROWS_LAST)
    gs = (p * (gp - delta)).astype(bf16)
    return dot(p.astype(bf16), go, PLAIN), dot(gs, q, PLAIN), dot(k, gs, FIRST_FIRST)


def remote_backward_kernel(
    out_at,
    info_ref,
    own_ref,
    oth_ref,
    kv_ref,
    seg_col_ref,
    seg_row_ref,
    kept_ref,
    other_ref,
    first_ref,
    second_ref,
    attn_ref,
    lse_ref,
    gkv_ref,
    gq_ref,
    delta_ref,
    go_ref,
    gk_acc,
    gv_acc,
):
    i = pl.program_id(0)
    core = info_ref[0]
    query_at = physical(i, core)

    @pl.when(i == 0)
    def _():
        gk_acc[...] = jnp.zeros_like(gk_acc)
        gv_acc[...] = jnp.zeros_like(gv_acc)

    wide = rows_of(lax.rem(i + 2 * core, 4), kept_ref, other_ref)
    go_ref[:, 0:192] = dot(wide, first_ref[:, out_at[0] : out_at[0] + 192], PLAIN).astype(bf16)
    go_ref[:, 192:384] = dot(wide, second_ref[:, out_at[1] : out_at[1] + 192], PLAIN).astype(bf16)
    for pair in range(3):
        columns = slice(pair * 128, pair * 128 + 128)
        product = (go_ref[:, columns].astype(f32) * attn_ref[:, columns].astype(f32)).T
        for half in range(2):
            delta_ref[2 * pair + half : 2 * pair + half + 1, :] = jnp.sum(
                product[half * 64 : half * 64 + 64], 0, keepdims=True
            )
    delta_ref[6:8, :] = jnp.zeros((2, TILE), f32)
    gq_ref[...] = jnp.zeros_like(gq_ref)

    def step(j, carry):
        key_at = pl.multiple_of(j * REMOTE_TILE, REMOTE_TILE)
        rows = pl.ds(key_at, REMOTE_TILE)
        bias = tile_bias(seg_col_ref[rows, :], seg_row_ref[...], 0, REMOTE_ROWS)
        for h in range(6):
            ref = own_ref if h < 3 else oth_ref
            q = ref[pl.ds(query_at, TILE), head_columns(h, 0)] * bf16(0.125)
            base = (h // 3) * 384 + (h % 3) * HEAD_DIM
            k = kv_ref[rows, base : base + HEAD_DIM]
            v = kv_ref[rows, base + 192 : base + 192 + HEAD_DIM]
            go = go_ref[:, h * HEAD_DIM : (h + 1) * HEAD_DIM]
            gv, gk, gq = backward_step(
                q, k, v, go, lse_ref[h : h + 1, :], delta_ref[h : h + 1, :], bias
            )
            gv_acc[h, rows, :] += gv
            gk_acc[h, rows, :] += gk
            gq_ref[h * HEAD_DIM : (h + 1) * HEAD_DIM, :] += gq
        return carry

    lax.fori_loop(info_ref[5 + i], REMOTE_ROWS // REMOTE_TILE, step, 0)

    @pl.when(i == pl.num_programs(0) - 1)
    def _():
        for h in range(6):
            base = (h // 3) * 384 + (h % 3) * HEAD_DIM
            gkv_ref[:, base : base + HEAD_DIM] = gk_acc[h].astype(bf16)
            gkv_ref[:, base + 192 : base + 192 + HEAD_DIM] = gv_acc[h].astype(bf16)


def remote_backward(info, own, oth, kv, seg_col, seg_row, wide, outs, attn, lse):
    out_at, (first, second) = outs
    rows = own.shape[0]
    return pl.pallas_call(
        functools.partial(remote_backward_kernel, out_at),
        grid_spec=pltpu.PrefetchScalarGridSpec(
            num_scalar_prefetch=1,
            grid=(rows // TILE,),
            in_specs=[
                whole(own.shape),
                whole(oth.shape),
                whole(kv.shape),
                whole(seg_col.shape),
                position_block(1),
                kept_block(wide[0].shape[1]),
                other_block(wide[0].shape[1]),
                whole(first.shape),
                whole(second.shape),
                physical_block(384),
                position_block(8),
            ],
            out_specs=[
                whole(kv.shape), position_block(384), position_block(8), physical_block(384)
            ],
            scratch_shapes=[
                pltpu.VMEM((6, REMOTE_ROWS, HEAD_DIM), f32),
                pltpu.VMEM((6, REMOTE_ROWS, HEAD_DIM), f32),
            ],
        ),
        out_shape=[
            jax.ShapeDtypeStruct(kv.shape, bf16),
            jax.ShapeDtypeStruct((384, rows), f32),
            jax.ShapeDtypeStruct((8, rows), f32),
            jax.ShapeDtypeStruct((rows, 384), bf16),
        ],
        compiler_params=PARAMS,
    )(info, own, oth, kv, seg_col, seg_row, *wide, first, second, attn, lse)


def local_backward_kernel(
    info_ref,
    own_ref,
    oth_ref,
    seg_col_ref,
    seg_row_ref,
    go_ref,
    lse_ref,
    delta_ref,
    gq_in,
    gown_ref,
    goth_ref,
    gq_acc,
    gk_acc,
    gv_acc,
):
    i = pl.program_id(0)
    core = info_ref[0]
    query_at = physical(i, core)

    @pl.when(i == 0)
    def _():
        gk_acc[...] = jnp.zeros_like(gk_acc)
        gv_acc[...] = jnp.zeros_like(gv_acc)

    gq_acc[...] = gq_in[...]

    def step(back, carry):
        j = i - back
        rows = pl.ds(physical(j, core), TILE)
        j_pos = pl.multiple_of(j * TILE, TILE)
        bias = tile_bias(
            seg_col_ref[pl.ds(j_pos, TILE), :], seg_row_ref[...], j * TILE, i * TILE
        )
        for h in range(6):
            ref = own_ref if h < 3 else oth_ref
            q = ref[pl.ds(query_at, TILE), head_columns(h, 0)] * bf16(0.125)
            k = ref[rows, head_columns(h, 1)]
            v = ref[rows, head_columns(h, 2)]
            go = go_ref[:, h * HEAD_DIM : (h + 1) * HEAD_DIM]
            gv, gk, gq = backward_step(
                q, k, v, go, lse_ref[h : h + 1, :], delta_ref[h : h + 1, :], bias
            )
            gv_acc[h, rows, :] += gv
            gk_acc[h, rows, :] += gk
            gq_acc[h * HEAD_DIM : (h + 1) * HEAD_DIM, :] += gq
        return carry

    lax.fori_loop(0, i - info_ref[1 + i] + 1, step, 0)
    for h in range(6):
        out = gown_ref if h < 3 else goth_ref
        block = gq_acc[h * HEAD_DIM : (h + 1) * HEAD_DIM, :].T * 0.125
        out[pl.ds(query_at, TILE), head_columns(h, 0)] = block.astype(bf16)

    @pl.when(i == pl.num_programs(0) - 1)
    def _():
        for h in range(6):
            out = gown_ref if h < 3 else goth_ref
            out[:, head_columns(h, 1)] = gk_acc[h].astype(bf16)
            out[:, head_columns(h, 2)] = gv_acc[h].astype(bf16)


def local_backward(info, own, oth, seg_col, seg_row, go, lse, delta, gq):
    rows = own.shape[0]
    return pl.pallas_call(
        local_backward_kernel,
        grid_spec=pltpu.PrefetchScalarGridSpec(
            num_scalar_prefetch=1,
            grid=(rows // TILE,),
            in_specs=[
                whole(own.shape),
                whole(oth.shape),
                whole(seg_col.shape),
                position_block(1),
                physical_block(384),
                position_block(8),
                position_block(8),
                position_block(384),
            ],
            out_specs=[whole(own.shape), whole(oth.shape)],
            scratch_shapes=[
                pltpu.VMEM((384, TILE), f32),
                pltpu.VMEM((6, rows, HEAD_DIM), f32),
                pltpu.VMEM((6, rows, HEAD_DIM), f32),
            ],
        ),
        out_shape=[
            jax.ShapeDtypeStruct(own.shape, bf16),
            jax.ShapeDtypeStruct(oth.shape, bf16),
        ],
        compiler_params=PARAMS,
    )(info, own, oth, seg_col, seg_row, go, lse, delta, gq)


def normalize(v):
    center = v - jnp.mean(v, -1, keepdims=True)
    scale = lax.rsqrt(jnp.mean(center * center, -1, keepdims=True) + EPSILON)
    return center * scale, scale


def norm_forward_kernel(rounded, base_ref, part_ref, received_ref, rows_ref, total_ref, normed_ref):
    total = base_ref[...].astype(f32) + (
        part_ref[...] + received_ref[...].astype(f32) + rows_ref[0:1, :]
    )
    if rounded:
        total = total.astype(bf16)
    total_ref[...] = total
    unit, _ = normalize(total.astype(f32))
    normed_ref[...] = (unit * rows_ref[1:2, :] + rows_ref[2:3, :]).astype(bf16)


def norm_forward(base, part, received, bias, gain, shift, rounded):
    rows, width = base.shape
    vectors = jnp.stack([bias, gain, shift])
    return pl.pallas_call(
        functools.partial(norm_forward_kernel, rounded),
        grid=(rows // TILE,),
        in_specs=[tile_of(width)] * 3 + [fixed(vectors.shape)],
        out_specs=[tile_of(width)] * 2,
        out_shape=[
            jax.ShapeDtypeStruct(base.shape, bf16 if rounded else f32),
            jax.ShapeDtypeStruct(base.shape, bf16),
        ],
        compiler_params=PARAMS,
    )(base, part, received, vectors)


def norm_backward_kernel(
    v_ref, part_ref, received_ref, above_ref, gain_ref, wide_ref, low_ref, sums_ref
):
    @pl.when(pl.program_id(0) == 0)
    def _():
        sums_ref[...] = jnp.zeros_like(sums_ref)

    grad = part_ref[...] + received_ref[...].astype(f32)
    unit, scale = normalize(v_ref[...].astype(f32))
    scaled = grad * gain_ref[...]
    back = scale * (
        scaled
        - jnp.mean(scaled, -1, keepdims=True)
        - unit * jnp.mean(scaled * unit, -1, keepdims=True)
    )
    total = above_ref[...].astype(f32) + back
    wide_ref[...] = total
    low = total.astype(bf16)
    low_ref[...] = low
    sums_ref[0:1, :] += jnp.sum(grad * unit, 0, keepdims=True)
    sums_ref[1:2, :] += jnp.sum(grad, 0, keepdims=True)
    sums_ref[2:3, :] += jnp.sum(low.astype(f32), 0, keepdims=True)


def norm_backward(v, part, received, above, gain):
    rows, width = v.shape
    return pl.pallas_call(
        norm_backward_kernel,
        grid=(rows // TILE,),
        in_specs=[tile_of(width)] * 4 + [fixed((1, width))],
        out_specs=[tile_of(width)] * 2 + [fixed((8, width))],
        out_shape=[
            jax.ShapeDtypeStruct(v.shape, f32),
            jax.ShapeDtypeStruct(v.shape, bf16),
            jax.ShapeDtypeStruct((8, width), f32),
        ],
        compiler_params=PARAMS,
    )(v, part, received, above, gain[None])


def both_rows(own):
    return jnp.concatenate([own, swap_core(own)], 0)


def split_sum(parts):
    half = parts[0][0].shape[0] // 2

    def partial(rows):
        return sum(dot(a[rows], b, ROWS_LAST) for a, b in parts)

    received = swap_core(partial(slice(half, None)).astype(bf16))
    return partial(slice(0, half)), received


def gelu_and_slope(v):
    c, a = 0.7978845608028654, 0.044715
    square = v * v
    t = jnp.tanh(c * v * (1.0 + a * square))
    half = 0.5 * (1.0 + t)
    slope = half + 0.5 * v * (1.0 - t * t) * (c * (1.0 + 3.0 * a * square))
    return v * half, slope


def units_forward_kernel(widths, kept_ref, other_ref, *refs):
    count = len(widths)
    ups, downs = refs[:count], refs[count : 2 * count]
    bias_ref, hidden_ref, slope_ref, part_ref, sent_ref = refs[2 * count :]
    x = rows_of(pl.program_id(0), kept_ref, other_ref)
    at, total = 0, None
    for width, up, down in zip(widths, ups, downs):
        columns = slice(at, at + width)
        value, slope = gelu_and_slope(dot(x, up[:, :width], PLAIN) + bias_ref[:, columns])
        value = value.astype(bf16)
        hidden_ref[:, columns] = value
        slope_ref[:, columns] = slope.astype(bf16)
        term = dot(value, down[...], ROWS_LAST)
        total = term if total is None else total + term
        at += width
    store_rows(pl.program_id(0), total, part_ref, sent_ref)


def units_forward(x, ups, downs, bias):
    rows, width = 2 * x[0].shape[0], x[0].shape[1]
    widths = [w.shape[1] for w in downs]
    units = sum(widths)
    return pl.pallas_call(
        functools.partial(units_forward_kernel, widths),
        grid=(rows // TILE,),
        in_specs=[KEPT_ROWS, SENT_ROWS]
        + [fixed(w.shape) for w in ups + downs]
        + [fixed((1, units))],
        out_specs=[tile_of(units), tile_of(units), KEPT_ROWS, SENT_ROWS],
        out_shape=[
            jax.ShapeDtypeStruct((rows, units), bf16),
            jax.ShapeDtypeStruct((rows, units), bf16),
            jax.ShapeDtypeStruct((rows // 2, width), f32),
            jax.ShapeDtypeStruct((rows // 2, width), bf16),
        ],
        compiler_params=PARAMS,
    )(*x, *ups, *downs, bias[None])


def units_backward_kernel(widths, kept_ref, other_ref, slope_ref, *refs):
    count = len(widths)
    ups, downs = refs[:count], refs[count : 2 * count]
    gpre_ref, part_ref, sent_ref, sums_ref = refs[2 * count :]

    @pl.when(pl.program_id(0) == 0)
    def _():
        sums_ref[...] = jnp.zeros_like(sums_ref)

    g = rows_of(pl.program_id(0), kept_ref, other_ref)
    at, total = 0, None
    for width, up, down in zip(widths, ups, downs):
        columns = slice(at, at + width)
        gpre = (dot(g, down[...], PLAIN) * slope_ref[:, columns].astype(f32)).astype(bf16)
        gpre_ref[:, columns] = gpre
        sums_ref[0:1, columns] += jnp.sum(gpre.astype(f32), 0, keepdims=True)
        term = dot(gpre, up[:, :width], ROWS_LAST)
        total = term if total is None else total + term
        at += width
    store_rows(pl.program_id(0), total, part_ref, sent_ref)


def units_backward(g, slopes, ups, downs):
    rows, width = 2 * g[0].shape[0], g[0].shape[1]
    units = slopes.shape[1]
    return pl.pallas_call(
        functools.partial(units_backward_kernel, [w.shape[1] for w in downs]),
        grid=(rows // TILE,),
        in_specs=[KEPT_ROWS, SENT_ROWS, tile_of(units)] + [fixed(w.shape) for w in ups + downs],
        out_specs=[tile_of(units), KEPT_ROWS, SENT_ROWS, fixed((8, units))],
        out_shape=[
            jax.ShapeDtypeStruct((rows, units), bf16),
            jax.ShapeDtypeStruct((rows // 2, width), f32),
            jax.ShapeDtypeStruct((rows // 2, width), bf16),
            jax.ShapeDtypeStruct((8, units), f32),
        ],
        compiler_params=PARAMS,
    )(*g, slopes, *ups, *downs)


def block_forward(h, normed, masks, weights, vectors, hook):
    info, seg_col, seg_row, seg_far_col, is_first_core = masks
    qkv, outs, up, down = weights
    _, _, out_bias, ln2_gain, ln2_shift, _, qkv_bias, up_bias = vectors
    normed = both_rows(hook(K.ROWS, normed))
    proj = [(dot(normed, qkv[n], PLAIN) + qkv_bias[n]).astype(bf16) for n in range(2)]
    half = normed.shape[0] // 2
    keys = jnp.concatenate([proj[1][:, 192:], proj[0][:, 192:]], 1)
    early = jnp.where(is_first_core, keys[:half], keys[half:])
    late = jnp.where(is_first_core, keys[half:], keys[:half])
    sent = jnp.concatenate([early[half - (REMOTE_ROWS - half) :], late], 0)
    far = lax.ppermute(hook(K.SENT, sent), TENSOR, [(0, 2), (1, 3)])
    proj = hook(K.ATTEND, proj)
    state = local_forward(info, proj[0], proj[1], seg_col, seg_row)
    far = hook(K.FAR, far)
    attn, lse, part, sent = remote_forward(
        info, proj[0], proj[1], far, seg_far_col, seg_row, *state, outs
    )
    received = hook(K.MIDDLE, swap_core(sent))
    middle, second = norm_forward(h, part, received, out_bias, ln2_gain, ln2_shift, False)
    second = hook(K.SECOND, [second, swap_core(second)])
    hidden, slopes, part, sent = units_forward(second, up, down, jnp.concatenate(up_bias))
    received = hook(K.HIDDEN, swap_core(sent))
    return (middle, part, received), (h, middle, normed, proj, far, attn, lse, second, hidden, slopes)


def block_backward(gy, masks, saved, weights, vectors, grads, hook):
    info, seg_col, seg_row, seg_far_col, is_first_core = masks
    qkv, outs, up, down = weights
    ln1_gain, ln2_gain = vectors[0], vectors[3]
    h, middle, normed, proj, far, attn, lse, second, hidden, slopes = saved
    wide = [gy, swap_core(gy)]
    gpre, part, sent, up_sums = units_backward(wide, slopes, up, down)
    wide, second = jnp.concatenate(wide, 0), jnp.concatenate(second, 0)
    grads[K.GPRE] = sent
    received = swap_core(sent)
    units = hidden.shape[1] // 2
    g_down = dot(wide, hidden, FIRST_FIRST).astype(bf16)
    g_up = dot(second, gpre, FIRST_FIRST).astype(bf16)
    grads[K.DOWN] = [g_down[:, :units], g_down[:, units:]]
    grads[K.UP] = [g_up[:, :units], g_up[:, units:]]
    received = hook(K.GPRE, after(received, g_down, g_up))
    gmid, gmr, sums2 = norm_backward(middle, part, received, gy, ln2_gain)
    mid_wide = hook(K.GMR, [gmr, swap_core(gmr)])
    gfar, gq, delta, gattn = remote_backward(
        info, proj[0], proj[1], far, seg_far_col, seg_row, mid_wide, outs, attn, lse
    )
    gnear = lax.ppermute(gfar, TENSOR, [(2, 0), (3, 1)])
    mid_wide = jnp.concatenate(mid_wide, 0)
    grads[K.OUT] = [
        dot(mid_wide, attn[:, n * 192 : n * 192 + 192], FIRST_FIRST).astype(bf16) for n in range(2)
    ]
    gproj = local_backward(info, proj[0], proj[1], seg_col, seg_row, gattn, lse, delta, gq)
    grads[K.GPROJ] = gproj[0]
    gproj = hook(K.GPROJ, gproj)
    half = normed.shape[0] // 2
    gnear = jnp.pad(gnear, ((2 * half - REMOTE_ROWS, 0), (0, 0)))
    gnear = jnp.concatenate(
        [
            jnp.where(is_first_core, gnear[:half], gnear[half:]),
            jnp.where(is_first_core, gnear[half:], gnear[:half]),
        ],
        0,
    )
    gproj = [
        (gproj[n].astype(f32) + jnp.pad(gnear[:, at : at + 384].astype(f32), ((0, 0), (192, 0))))
        .astype(bf16)
        for n, at in ((0, 384), (1, 0))
    ]
    g_qkv_bias = [jnp.sum(g.astype(f32), 0) for g in gproj]
    grads[K.QKV] = [dot(normed, gproj[n], FIRST_FIRST).astype(bf16) for n in range(2)]
    grads[K.MARK] = grads[K.QKV][1]
    part, received = split_sum([(gproj[0], qkv[0]), (gproj[1], qkv[1])])
    received = hook(K.GNORMED, received)
    _, gin, sums1 = norm_backward(h, part, received, gmid, ln1_gain)
    rows_grads = [sums1[0], sums1[1], sums2[2], sums2[0], sums2[1]]
    g_up_bias = [up_sums[0, :units], up_sums[0, units:]]
    return gin, rows_grads, sums1[2], (g_qkv_bias, g_up_bias)


class Stages:
    def __init__(self):
        self.makers, self.made = {}, {}

    def __getitem__(self, key):
        if key not in self.made:
            self.made[key] = self.makers[key]()
        return self.made[key]

    def hook(self, plan):
        def tie(name, value):
            keys = plan.get(name, ())
            return after(value, *[self[key] for key in keys]) if keys else value

        return tie


def section_first(v, is_leading):
    half = v.shape[-1] // 2
    return jnp.where(is_leading, v, jnp.concatenate([v[..., half:], v[..., :half]], -1))


def body(
    tokens,
    segments,
    cotangent,
    ln1_gain,
    ln1_shift,
    qkv_weight,
    qv_bias,
    out_weight,
    out_bias,
    ln2_gain,
    ln2_shift,
    up_weight,
    up_bias,
    down_weight,
    down_bias,
):
    section = lax.axis_index(SECTION)
    is_leading = section == 0
    tensor = lax.axis_index(TENSOR)
    core = lax.rem(tensor, 2)
    chip = tensor // 2
    dp = lax.axis_index(DP)
    dp_size = lax.axis_size(DP)
    place = dp.astype(jnp.int32).reshape(1)
    share = ln1_gain.shape[1]
    features = share * dp_size
    local_width = qkv_weight.shape[3]
    local_units = up_weight.shape[2]

    row = jnp.concatenate(
        [
            ln1_gain[0],
            ln1_shift[0],
            out_bias[0],
            ln2_gain[0],
            ln2_shift[0],
            down_bias[0],
            qv_bias[0].reshape(-1),
            up_bias[0].reshape(-1),
        ]
    )[None]
    other_row = swap_section(row)
    rows = jnp.where(
        is_leading, jnp.concatenate([row, other_row], 1), jnp.concatenate([other_row, row], 1)
    )
    rows = jnp.concatenate([rows, swap_chip(rows)], 1)
    if dp_size == 4:
        pieces = [rows] + [shift_dp(rows, k) for k in range(1, dp_size)]
        rows = jnp.zeros((dp_size,) + rows.shape[1:], rows.dtype)
        for k in range(dp_size):
            rows = lax.dynamic_update_slice_in_dim(
                rows, pieces[k], lax.rem(dp + dp_size - k, dp_size), 0
            )
    else:
        rows = lax.all_gather(rows, DP, axis=0, tiled=True)
    length = row.shape[1]
    rows = rows.reshape(dp_size, 2, 2, length).astype(f32)
    qv_share = local_width // dp_size
    up_share = local_units // dp_size

    def vectors_of(b):
        plain = [rows[:, 0, b, n * share : (n + 1) * share].reshape(-1) for n in range(6)]
        qkv_bias, up_biases = [], []
        for n in range(2):
            at = 6 * share
            query = rows[:, n, b, at : at + qv_share].reshape(-1)
            value = rows[:, n, b, at + qv_share : at + 2 * qv_share].reshape(-1)
            qkv_bias.append(jnp.concatenate([query, jnp.zeros_like(query), value]))
            up_biases.append(rows[:, n, b, at + 2 * qv_share :].reshape(-1))
        up_biases[1] = section_first(up_biases[1], is_leading)
        return tuple(plain) + (qkv_bias, up_biases)

    vectors = [vectors_of(b) for b in range(2)]

    qkv_columns = 3 * local_width
    out_at = -(-qkv_columns // 128) * 128
    stages = Stages()
    first_slab = jnp.concatenate(
        [
            qkv_weight[0].reshape(share, qkv_columns),
            jnp.zeros((share, out_at - qkv_columns), bf16),
            out_weight[0].T,
        ],
        1,
    )
    slabs = {K.FIRST: first_slab, K.UP: up_weight[0], K.DOWN: down_weight[0].T}
    others = {K.FIRST: swap_section(first_slab)}
    for name in (K.UP, K.DOWN):
        others[name] = swap_section(after(slabs[name], others[K.FIRST]))

    def describe(b, name):
        def pick():
            return jnp.where(section == b, slabs[name], others[name])

        stages.makers[K.PICK, b, name] = pick
        stages.makers[K.DP, b, name] = lambda: gather_dp(stages[K.PICK, b, name])
        if name == K.FIRST:
            stages.makers[K.CHIP, b, name] = lambda: swap_chip(stages[K.DP, b, name])
            return
        half = local_units // 2

        def my_half():
            full = stages[K.DP, b, name]
            return jnp.where(is_leading, full[:, :half], full[:, half:])

        stages.makers[K.CHIP, b, name] = lambda: swap_chip(my_half())
        stages.makers[K.SECTION, b, name] = lambda: swap_section(stages[K.CHIP, b, name])
        stages.makers[K.ALL, b, name] = lambda: [
            stages[K.DP, b, name], stages[K.CHIP, b, name], stages[K.SECTION, b, name]
        ]

    for b in range(2):
        for name in slabs:
            describe(b, name)

    def weights_of(b):
        first = [stages[K.DP, b, K.FIRST], stages[K.CHIP, b, K.FIRST]]
        return (
            [w[:, :qkv_columns] for w in first],
            ((out_at, out_at), first),
            stages[K.ALL, b, K.UP],
            stages[K.ALL, b, K.DOWN],
        )

    seg = jnp.where(is_leading, segments[0, 0], segments[1, 0])
    near_len = seg.shape[0] // 2
    seg_near = lax.dynamic_slice_in_dim(seg, chip * near_len, near_len, 0)
    seg_far = seg[near_len - REMOTE_ROWS : near_len]
    heads_of = seg_near[::TILE]
    start = jnp.sum((seg_near[None, :] < heads_of[:, None]).astype(jnp.int32), 1)
    far_start = jnp.sum((seg_far < seg_far[-1]).astype(jnp.int32))
    crosses = (heads_of == seg_far[-1]) & (chip == 1)
    info = jnp.concatenate(
        [
            core.astype(jnp.int32).reshape(1),
            start // TILE,
            jnp.where(crosses, far_start // REMOTE_TILE, REMOTE_ROWS // REMOTE_TILE),
        ]
    ).astype(jnp.int32)
    masks = (info, seg_near[:, None], seg_near[None, :], seg_far[:, None], core == 0)

    h = jnp.where(is_leading, tokens[0, 0], tokens[1, 0])
    normed = normalize(h.astype(f32))[0] * vectors[0][0] + vectors[0][1]
    normed = normed.astype(bf16)
    outs, saved, weights, back = [], [], [], [None, None]
    stages.makers[K.OUT, 0] = lambda: lax.ppermute(outs[0], SECTION, [(1, 0)])
    stages.makers[K.OUT, 1] = lambda: lax.ppermute(outs[1], SECTION, [(0, 1)])
    stages.makers[K.BACK, 1] = lambda: lax.ppermute(back[1], SECTION, [(0, 1)])
    stages.makers[K.BACK, 0] = lambda: lax.ppermute(back[0], SECTION, [(1, 0)])
    plans = (
        {
            K.ATTEND: ((K.DP, 0, K.UP), (K.PICK, 0, K.DOWN)),
            K.FAR: ((K.CHIP, 0, K.UP), (K.DP, 0, K.DOWN)),
            K.MIDDLE: ((K.SECTION, 0, K.UP), (K.DP, 1, K.FIRST)),
            K.SECOND: ((K.CHIP, 0, K.DOWN), (K.DP, 1, K.UP)),
            K.HIDDEN: ((K.CHIP, 1, K.FIRST), (K.DP, 1, K.DOWN)),
        },
        {
            K.SENT: ((K.CHIP, 1, K.UP),),
            K.FAR: ((K.SECTION, 1, K.UP), (K.CHIP, 1, K.DOWN)),
        },
    )
    for b in range(2):
        weights.append(weights_of(b))
        (middle, part, received), kept = block_forward(
            h, normed, masks, weights[b], vectors[b], stages.hook(plans[b])
        )
        saved.append(kept)
        bias = vectors[b][5]
        if b == 0:
            h, normed = norm_forward(
                middle, part, received, bias, vectors[1][0], vectors[1][1], True
            )
            outs.append(h)
        else:
            outs.append((middle + (part + received.astype(f32) + bias)).astype(bf16))

    gy = jnp.where(is_leading, cotangent[0, 0], cotangent[1, 0])
    above_sum = jnp.sum(gy.astype(f32), 0)
    row_grads = [None, None]
    unit_grads = [None, None]
    grads = [{}, {}]

    def not_before(b, received):
        return after(received, grads[0][K.GPRE]) if b == 1 else received

    def halves(v):
        return v[:, : v.shape[1] // 2], v[:, v.shape[1] // 2 :]

    def describe_back(b):
        parts = (K.DOWN, K.UP)

        def section_half():
            theirs, others = [], []
            for name in parts:
                own, other = grads[b][name]
                low, high = halves(own)
                theirs.append(jnp.where(is_leading, high, low))
                others.append(halves(other)[1])
            received = swap_section(jnp.concatenate(theirs + others, 1))
            return after(received, grads[0][K.GPROJ]) if b == 0 else received

        def chip_half():
            mine = jnp.concatenate([halves(grads[b][name][1])[0] for name in parts], 1)
            received = after(stages[K.GSECTION, b], grads[b][K.MARK])
            total = mine.astype(f32) + halves(received)[1].astype(f32)
            return not_before(b, swap_chip(total.astype(bf16)))

        def units():
            mine = []
            for name in parts:
                low, high = halves(grads[b][name][0])
                mine.append(jnp.where(is_leading, low, high))
            total = jnp.concatenate(mine, 1).astype(f32)
            total = total + halves(stages[K.GSECTION, b])[0].astype(f32)
            total = total + stages[K.GCHIP, b, K.UNITS].astype(f32)
            return total.astype(bf16)

        def joined(n):
            return jnp.concatenate([grads[b][K.OUT][n], grads[b][K.QKV][n]], 1)

        def heads():
            total = joined(0).astype(f32) + stages[K.GCHIP, b, K.HEADS].astype(f32)
            return total.astype(bf16)

        stages.makers[K.GSECTION, b] = section_half
        stages.makers[K.GCHIP, b, K.UNITS] = chip_half
        stages.makers[K.GCHIP, b, K.HEADS] = lambda: not_before(b, swap_chip(joined(1)))
        stages.makers[K.PICK, b, K.UNITS] = units
        stages.makers[K.PICK, b, K.HEADS] = heads
        stages.makers[K.GDP, b, K.UNITS] = lambda: scatter_dp(stages[K.PICK, b, K.UNITS])
        stages.makers[K.GDP, b, K.HEADS] = lambda: scatter_dp(stages[K.PICK, b, K.HEADS])

    for b in range(2):
        describe_back(b)
    plans = (
        {
            K.GPRE: ((K.GCHIP, 1, K.HEADS),),
            K.GMR: ((K.GCHIP, 1, K.UNITS),),
            K.GPROJ: ((K.GSECTION, 0), (K.GDP, 1, K.HEADS)),
            K.GNORMED: ((K.GCHIP, 0, K.UNITS), (K.GDP, 1, K.UNITS), (K.BACK, 1), (K.OUT, 0)),
        },
        {
        },
    )
    for b in (1, 0):
        gy, plain_grads, below_sum, unit_grads[b] = block_backward(
            gy, masks, saved[b], weights[b], vectors[b], grads[b], stages.hook(plans[b])
        )
        back[b] = gy
        row_grads[b] = plain_grads + [above_sum]
        above_sum = below_sum

    pair = stages[K.GDP, 0, K.HEADS], stages[K.GDP, 1, K.HEADS]
    keep = jnp.where(is_leading, pair[0], pair[1])
    give = jnp.where(is_leading, pair[1], pair[0])
    g_heads = keep.astype(f32) + swap_section(give).astype(f32)
    g_out, g_qkv = g_heads[:, :local_width], g_heads[:, local_width:]
    pair = stages[K.GDP, 0, K.UNITS], stages[K.GDP, 1, K.UNITS]
    keep = jnp.where(is_leading, pair[0], pair[1])
    give = jnp.where(is_leading, pair[1], pair[0])
    keep, other = keep.astype(f32), swap_section(give).astype(f32)
    half = local_units // 2

    def in_order(at):
        mine, theirs = keep[:, at : at + half], other[:, at : at + half]
        return jnp.concatenate(
            [jnp.where(is_leading, mine, theirs), jnp.where(is_leading, theirs, mine)], 1
        )

    g_down, g_up = in_order(0), in_order(half)

    plain = jnp.stack([jnp.concatenate(row_grads[b]) for b in range(2)])
    plain = after(plain, stages[K.PICK, 0, K.UNITS])
    plain = plain + swap_core(plain)
    units = [
        jnp.stack(
            [
                jnp.concatenate(
                    [
                        unit_grads[b][0][n],
                        unit_grads[b][1][n]
                        if n == 0
                        else section_first(unit_grads[b][1][n], is_leading),
                    ]
                )
                for b in range(2)
            ]
        )
        for n in range(2)
    ]
    swapped = swap_chip(jnp.concatenate([plain, units[1]], 1))
    plain_width = plain.shape[1]
    total = jnp.concatenate([plain, units[0]], 1) + swapped
    total = after(
        total, stages[K.PICK, 0, K.HEADS], stages[K.GDP, 0, K.UNITS], stages[K.OUT, 1]
    )
    total = total_dp(total)
    keep = jnp.where(is_leading, total[0], total[1])
    give = jnp.where(is_leading, total[1], total[0])
    total = keep + swap_section(give[None])[0]

    def mine(vector):
        part = vector.shape[0] // dp_size
        return lax.dynamic_slice_in_dim(vector, dp * part, part, 0)

    shares = [mine(total[n * features : (n + 1) * features]) for n in range(6)]
    unit_total = total[plain_width:]
    g_query = mine(unit_total[:local_width])
    g_value = mine(unit_total[2 * local_width : 3 * local_width])
    g_up_bias = mine(unit_total[3 * local_width :])

    def exchanged(name, pair):
        own = jnp.where(is_leading, pair[0], pair[1])
        other = jnp.where(is_leading, stages[name, 0], stages[name, 1])
        return jnp.stack(
            [jnp.where(is_leading, own, other), jnp.where(is_leading, other, own)]
        )[None, :, None]

    return (
        exchanged(K.OUT, outs),
        exchanged(K.BACK, back),
        shares[0][None],
        shares[1][None],
        g_qkv.reshape(1, share, 3, local_width),
        jnp.stack([g_query, g_value])[None, :, None],
        g_out.T[None],
        shares[2][None],
        shares[3][None],
        shares[4][None],
        g_up[None],
        g_up_bias[None, None],
        g_down.T[None],
        shares[5][None],
    )


def solution(mesh):
    placed = (
        P(None, DP, TENSOR, None),
        P(None, DP, None),
        P(None, DP, TENSOR, None),
        P(SECTION, DP),
        P(SECTION, DP),
        P(SECTION, DP, None, TENSOR),
        P(SECTION, None, TENSOR, DP),
        P(SECTION, TENSOR, DP),
        P(SECTION, DP),
        P(SECTION, DP),
        P(SECTION, DP),
        P(SECTION, DP, TENSOR),
        P(SECTION, TENSOR, DP),
        P(SECTION, TENSOR, DP),
        P(SECTION, DP),
    )
    return jax.shard_map(
        body,
        mesh=mesh,
        in_specs=placed,
        out_specs=(
            P(SECTION, None, DP, TENSOR, None),
            P(SECTION, None, DP, TENSOR, None),
            P(SECTION, DP),
            P(SECTION, DP),
            P(SECTION, DP, None, TENSOR),
            P(SECTION, None, TENSOR, DP),
            P(SECTION, TENSOR, DP),
            P(SECTION, DP),
            P(SECTION, DP),
            P(SECTION, DP),
            P(SECTION, DP, TENSOR),
            P(SECTION, TENSOR, DP),
            P(SECTION, TENSOR, DP),
            P(SECTION, DP),
        ),
        check_vma=False,
    )
```
